32 devices in a mesh: groups: 2 (over y), src: 16 (over z, x, core).
Axes of the slice: x: 2, y: 2, z: 4, core: 2. Of those that a mesh axis runs over, the one named last changes fastest.
Arguments:
- src_latent: float32 [64, 8192], P(None, ('groups', 'src')), parts along dimension 1, may hold values from -0.75 to 0.75
- src_potential: float32 [2, 8192], P(None, ('groups', 'src')), parts along dimension 1, may hold values from 0.3 to 0.7
- tgt_latent: float32 [64, 4096], P(None, ('groups', 'src')), parts along dimension 1, may hold values from -0.75 to 0.75
- tgt_potential: float32 [2, 4096], P(None, ('groups', 'src')), parts along dimension 1, may hold values from 0.3 to 0.7
Outputs:
- grad_src: float32 [64, 8192], P(None, ('groups', 'src')), parts along dimension 1
- grad_tgt: float32 [64, 4096], P(None, ('groups', 'src')), parts along dimension 1
The draws below stay inside these ranges and needn't reach their ends.
There are 2 independent parts, one for each index of `groups`. The reference program is written for one: setup_inputs(seed, part) draws one part's arguments, and reference() takes and returns one part's arrays. A program takes and returns all parts, laid end to end along the dimension named above; each array names one. Nothing has to cross between parts.
All inputs are finite; a program needn't handle non-finite values.
Results may differ from the reference program's by a relative error of at most 0.0003.
Values sent between devices are 32-bit elements; how exact they have to be, the bound alone decides.
No kernel may reach another device: no remote copies, remote signals or barrier semaphores. Data moves between devices by JAX's collectives and lax.ppermute only.
A program may use at most 64 MiB of HBM per device.

```python
import math
import jax
import jax.numpy as jnp
from jax import lax

D = 64
NS = 4096
NT = 2048


def level_of(rng, shape, cuts, least, high):
    loudness, own = 1.0, jax.random.fold_in(rng, 6)
    for position, parts in cuts:
        draws = jnp.exp(jax.random.uniform(jax.random.fold_in(own, position), (parts,), jnp.float32, least / len(cuts), high / len(cuts)))
        loudness = loudness * jnp.repeat(draws, shape[position] // parts).reshape([-1 if axis == position else 1 for axis in range(len(shape))])
    return loudness


def centred(rng, shape, spread, most, shards=(), held_as=jnp.bfloat16):
    loudness = level_of(rng, shape, shards, -0.22, 0.18) if shards else 1.0
    array = jax.random.normal(rng, shape, jnp.float32) * spread * loudness
    return jnp.minimum(jnp.maximum(array, -most), most).astype(held_as)


def setup_inputs(seed: int = 0, part: int = 0) -> dict:
    splits = jax.random.split(jax.random.key(seed), 5)
    own_keys = jax.random.split(jax.random.fold_in(splits[4], part), 5)
    src_latent = centred(own_keys[0], (D, NS), 0.125, 0.75, ((1, 16),), jnp.float32)
    src_potential = jnp.clip(0.3 + 0.39999998 * jax.random.uniform(own_keys[1], (2, NS), jnp.float32) ** level_of(own_keys[1], (2, NS), ((1, 16),), -0.2, 0.2), 0.3, 0.7)
    tgt_latent = centred(own_keys[2], (D, NT), 0.125, 0.75, ((1, 16),), jnp.float32)
    tgt_potential = jnp.clip(0.3 + 0.39999998 * jax.random.uniform(own_keys[3], (2, NT), jnp.float32) ** level_of(own_keys[3], (2, NT), ((1, 16),), -0.2, 0.2), 0.3, 0.7)
    return {"src_latent": src_latent, "src_potential": src_potential, "tgt_latent": tgt_latent, "tgt_potential": tgt_potential}


epsilon = 0.1
highest = lax.Precision.HIGHEST


def pair_kernel(left_lat, left_pot, left_first, right_lat, right_pot, right_first, self_pair):
    inner_prod = lax.dot_general(left_lat, right_lat, (((0,), (0,)), ((), ())), precision=highest, preferred_element_type=jnp.float32)
    pair_cost = 0.5 * jnp.sum(left_lat * left_lat, 0)[:, None] + 0.5 * jnp.sum(right_lat * right_lat, 0)[None, :] - inner_prod
    weight = jnp.exp((left_pot[:, None] + right_pot[None, :] - pair_cost) / epsilon)
    if self_pair:
        rows_id = left_first + lax.iota(jnp.int32, left_lat.shape[1])
        cols_id = right_first + lax.iota(jnp.int32, right_lat.shape[1])
        weight = jnp.where(rows_id[:, None] == cols_id[None, :], jnp.float32(0.0), weight)
    return weight


def sweep_pairs(left_lat, left_pot, piece_lat, piece_pot, self_pair, want_right):
    piece_count = piece_lat.shape[1]
    block_width = math.gcd(piece_count, 512)
    block_total = piece_count // block_width

    def block_step(running, block_index):
        block_begin = (block_index * block_width).astype(jnp.int32)
        block_cols = lax.dynamic_slice_in_dim(piece_lat, block_begin, block_width, 1)
        block_pot = lax.dynamic_slice_in_dim(piece_pot, block_begin, block_width, 0)
        weight = pair_kernel(left_lat, left_pot, jnp.int32(0), block_cols, block_pot, block_begin, self_pair)
        mixed_sum = lax.dot_general(block_cols, weight, (((1,), (1,)), ((), ())), precision=highest, preferred_element_type=jnp.float32)
        running = running + left_lat * jnp.sum(weight, 1)[None, :] - mixed_sum
        if want_right:
            back_sum = jnp.dot(left_lat, weight, precision=highest, preferred_element_type=jnp.float32)
            return running, block_cols * jnp.sum(weight, 0)[None, :] - back_sum
        return running, None

    running, right_terms = lax.scan(block_step, jnp.zeros(left_lat.shape, jnp.float32), jnp.arange(block_total, dtype=jnp.int32))
    if want_right:
        right_terms = jnp.transpose(right_terms, (1, 0, 2)).reshape(left_lat.shape[0], piece_count)
    return running, right_terms


def reference(src_latent, src_potential, tgt_latent, tgt_potential):
    cross_x, cross_y = sweep_pairs(src_latent, src_potential[0], tgt_latent, tgt_potential[0], False, True)
    self_x, unused_src = sweep_pairs(src_latent, src_potential[1], src_latent, src_potential[1], True, False)
    self_y, unused_tgt = sweep_pairs(tgt_latent, tgt_potential[1], tgt_latent, tgt_potential[1], True, False)
    grad_src = cross_x / NT - self_x / NS
    grad_tgt = cross_y / NS - self_y / NT
    return grad_src, grad_tgt
```

```python
import functools
import math

import jax
import jax.numpy as jnp
from jax import lax
from jax.experimental import pallas as pl
from jax.experimental.pallas import tpu as pltpu
from jax.sharding import PartitionSpec as P

SCALE = math.log2(math.e) / 0.1
LANES = 128
f32 = jnp.float32
bf16 = jnp.bfloat16


def split(value):
    high = value.astype(bf16).astype(f32)
    return high, value - high


def pack_kernel(slabs, feats, src_ref, srcp_ref, tgt_ref, tgtp_ref, out_ref):
    src_slabs = src_ref.shape[1] // LANES
    out_ref[slabs * feats :, :] = jnp.zeros((out_ref.shape[0] - slabs * feats, LANES), f32)
    for slab in range(slabs):
        ref, pot, at = (src_ref, srcp_ref, slab) if slab < src_slabs else (tgt_ref, tgtp_ref, slab - src_slabs)
        cols = slice(at * LANES, (at + 1) * LANES)
        out_ref[slab * feats : (slab + 1) * feats, :] = ref[:, cols]
        for which in range(2):
            row = slabs * feats + which * slabs + slab
            out_ref[row : row + 1, :] = pot[which : which + 1, cols]


def pair_kernel(shape, num_rows, num_cols, own, totals, *refs):
    feats, src_slabs, tgt_slabs = shape
    slabs = src_slabs + tgt_slabs
    rows, cols = refs[:num_rows], refs[num_rows : num_rows + num_cols]
    rest = refs[num_rows + num_cols :]
    keep_ref, send_ref, lhs_ref, rvec_ref = rest[-4:]
    prev = rest[:-4]

    def cell_terms(ref, slab):
        value = ref[slab * feats : (slab + 1) * feats, :]
        norm = 0.5 * jnp.sum(value * value, 0, keepdims=True)
        pots = [
            SCALE * (ref[slabs * feats + which * slabs + slab :][:1, :] - norm)
            for which in range(2)
        ]
        return value, pots

    def place(row, slab):
        if slab < src_slabs:
            return (row * src_slabs + slab) * LANES
        return (num_rows * src_slabs + row * tgt_slabs + slab - src_slabs) * LANES

    for row in range(num_rows):
        for slab in range(slabs):
            value, pots = cell_terms(rows[row], slab)
            high, low = split(value * SCALE)
            high, low = high.astype(bf16), low.astype(bf16)
            at = slice(place(row, slab), place(row, slab) + LANES)
            lhs_ref[0:feats, at] = high
            lhs_ref[feats : 2 * feats, at] = high
            lhs_ref[2 * feats : 3 * feats, at] = low
            lhs_ref[3 * feats :, at] = low
            for which in range(2):
                rvec_ref[which : which + 1, at] = pots[which]

    groups = []
    for kind, first, last in ((0, 0, src_slabs), (1, src_slabs, slabs)):
        members = [(col, slab) for col in range(num_cols) for slab in range(first, last)]
        width = 2
        for at in range(0, len(members), width):
            groups.append((kind, members[at : at + width]))

    prepared = []
    for kind, members in groups:
        trans, values, vecs = [], [], []
        for col, slab in members:
            value, pots = cell_terms(cols[col], slab)
            high, low = split(value)
            mid, least = split(low)
            both = jnp.concatenate([high, low], 0).T.astype(bf16)
            trans.append(jnp.concatenate([both, both], 1))
            stack = jnp.concatenate([high, mid, least, jnp.ones((16, LANES), f32)], 0)
            values.append(stack.astype(bf16))
            vecs.append(jnp.concatenate(pots + [jnp.zeros((6, LANES), f32)], 0).T)
        value = jnp.concatenate(values, 1)
        prepared.append(
            (kind, members, jnp.concatenate(trans, 0), jnp.concatenate([value, value], 1), jnp.concatenate(vecs, 0))
        )

    src_width = num_rows * src_slabs * LANES
    tgt_width = num_rows * tgt_slabs * LANES
    tile = 256
    results = {}
    for begin in range(0, src_width + tgt_width, tile):
        row_kind = 0 if begin < src_width else 1
        at = slice(begin, begin + tile)
        sums = [None, None]
        for kind, members, trans, value, vecs in prepared:
            which = 1 if kind == row_kind else 0
            power = jnp.dot(trans, lhs_ref[:, at], preferred_element_type=f32)
            power = power + (rvec_ref[which : which + 1, at] + vecs[:, which : which + 1])
            weight = jnp.exp2(power)
            if own and kind == row_kind:
                for pos, (col, slab) in enumerate(members):
                    if col == 0:
                        spot = place(0, slab)
                        if begin <= spot < begin + tile:
                            row_id = lax.broadcasted_iota(jnp.int32, weight.shape, 0) - pos * LANES
                            col_id = lax.broadcasted_iota(jnp.int32, weight.shape, 1) - (spot - begin)
                            same = (row_id == col_id) & (row_id >= 0) & (row_id < LANES)
                            weight = jnp.where(same, 0.0, weight)
            high, low = split(weight)
            both = jnp.concatenate([high.astype(bf16), low.astype(bf16)], 0)
            part = jnp.dot(value, both, preferred_element_type=f32)
            sums[kind] = part if sums[kind] is None else sums[kind] + part
        mixed = [s[0:feats] + s[feats : 2 * feats] + s[2 * feats : 3 * feats] for s in sums]
        mass = [s[3 * feats : 3 * feats + 1] for s in sums]
        sign = 1.0 if row_kind == 0 else -1.0
        inv = [sign / totals[0], sign / totals[1]]
        own_mass = mass[1] * inv[1] - mass[0] * inv[0]
        own_mixed = mixed[1] * inv[1] - mixed[0] * inv[0]
        for half in range(tile // LANES):
            spot = begin + half * LANES
            if row_kind == 0:
                row, slab = divmod(spot // LANES, src_slabs)
            else:
                row, slab = divmod((spot - src_width) // LANES, tgt_slabs)
                slab += src_slabs
            piece = slice(half * LANES, (half + 1) * LANES)
            value = rows[row][slab * feats : (slab + 1) * feats, :]
            grad = value * own_mass[:, piece] - own_mixed[:, piece]
            ref = (keep_ref, send_ref)[row % 2]
            out_at = slice(((row // 2) * slabs + slab) * LANES, ((row // 2) * slabs + slab + 1) * LANES)
            if prev:
                grad = grad + prev[row % 2][:, out_at]
            ref[:, out_at] = grad


def pair_terms(rows, cols, shape, own, totals, prev=()):
    feats, src_slabs, tgt_slabs = shape
    slabs = src_slabs + tgt_slabs
    out = jax.ShapeDtypeStruct((feats, len(rows) // 2 * slabs * LANES), f32)
    vmem = pl.BlockSpec(memory_space=pltpu.VMEM)
    args = [*rows, *cols, *prev]
    pairs = len(rows) * len(cols) * (slabs * LANES) ** 2
    return pl.pallas_call(
        functools.partial(pair_kernel, shape, len(rows), len(cols), own, totals),
        out_shape=(out, out),
        in_specs=[vmem] * len(args),
        out_specs=(vmem, vmem),
        scratch_shapes=[
            pltpu.VMEM((4 * feats, len(rows) * slabs * LANES), bf16),
            pltpu.VMEM((8, len(rows) * slabs * LANES), f32),
        ],
        compiler_params=pltpu.CompilerParams(vmem_limit_bytes=32 * 2**20),
        cost_estimate=pl.CostEstimate(flops=pairs * 1300, bytes_accessed=4 * 2**20, transcendentals=pairs),
    )(*args)


def body(src_latent, src_potential, tgt_latent, tgt_potential):
    feats, src_count = src_latent.shape
    tgt_count = tgt_latent.shape[1]
    src_slabs, tgt_slabs = src_count // LANES, tgt_count // LANES
    shape = (feats, src_slabs, tgt_slabs)
    slabs = src_slabs + tgt_slabs
    devices = lax.axis_size("src")
    totals = (src_count * devices, tgt_count * devices)
    pot_rows = -(-2 * slabs // 8) * 8
    vmem = pl.BlockSpec(memory_space=pltpu.VMEM)
    packed = pl.pallas_call(
        functools.partial(pack_kernel, slabs, feats),
        out_shape=jax.ShapeDtypeStruct((slabs * feats + pot_rows, LANES), f32),
        in_specs=[vmem] * 4,
        out_specs=vmem,
    )(src_latent, src_potential, tgt_latent, tgt_potential)

    def swap(value, bits):
        return lax.ppermute(value, "src", [(i, i ^ bits) for i in range(devices)])

    rows = [packed] + [swap(packed, k) for k in (1, 2, 3)]
    cols = [packed] + [swap(packed, k) for k in range(4, devices, 4)]
    prev = ()
    for at in range(0, len(cols), 4):
        prev = pair_terms(rows, cols[at : at + 4], shape, at == 0, totals, prev)
    keep, send = prev
    wide = slabs * LANES
    near = swap(send, 1)
    far = swap(keep[:, wide:] + near[:, wide:], 2)
    grad = keep[:, :wide] + near[:, :wide] + far
    return grad[:, :src_count], grad[:, src_count:]


def solution(mesh):
    spec = P(None, ("groups", "src"))
    return jax.shard_map(body, mesh=mesh, in_specs=(spec,) * 4, out_specs=(spec, spec), check_vma=False)
```

```python
import functools
import math

import jax
import jax.numpy as jnp
from jax import lax
from jax.experimental import pallas as pl
from jax.experimental.pallas import tpu as pltpu
from jax.sharding import PartitionSpec as P

SCALE = math.log2(math.e) / 0.1
LANES = 128
f32 = jnp.float32
bf16 = jnp.bfloat16


def split(value):
    high = value.astype(bf16).astype(f32)
    return high, value - high


def pack_kernel(slabs, feats, src_ref, srcp_ref, tgt_ref, tgtp_ref, out_ref):
    src_slabs = src_ref.shape[1] // LANES
    out_ref[slabs * feats :, :] = jnp.zeros((out_ref.shape[0] - slabs * feats, LANES), f32)
    for slab in range(slabs):
        ref, pot, at = (src_ref, srcp_ref, slab) if slab < src_slabs else (tgt_ref, tgtp_ref, slab - src_slabs)
        cols = slice(at * LANES, (at + 1) * LANES)
        out_ref[slab * feats : (slab + 1) * feats, :] = ref[:, cols]
        for which in range(2):
            row = slabs * feats + which * slabs + slab
            out_ref[row : row + 1, :] = pot[which : which + 1, cols]


def pair_kernel(shape, num_rows, num_cols, own, totals, *refs):
    feats, src_slabs, tgt_slabs = shape
    slabs = src_slabs + tgt_slabs
    rows, cols = refs[:num_rows], refs[num_rows : num_rows + num_cols]
    prev = refs[num_rows + num_cols : -num_rows - 2]
    outs, lhs_ref, rvec_ref = refs[-num_rows - 2 : -2], refs[-2], refs[-1]

    def cell_terms(ref, slab):
        value = ref[slab * feats : (slab + 1) * feats, :]
        norm = 0.5 * jnp.sum(value * value, 0, keepdims=True)
        first = slabs * feats + slab
        pots = [SCALE * (ref[first + which * slabs : first + which * slabs + 1, :] - norm) for which in range(2)]
        return value, pots

    row_slabs = [(row, slab) for row in range(num_rows) for slab in range(src_slabs)]
    src_width = len(row_slabs) * LANES
    row_slabs += [(row, slab) for row in range(num_rows) for slab in range(src_slabs, slabs)]
    for place, (row, slab) in enumerate(row_slabs):
        value, pots = cell_terms(rows[row], slab)
        high, low = split(value * SCALE)
        high, low = high.astype(bf16), low.astype(bf16)
        at = slice(place * LANES, (place + 1) * LANES)
        lhs_ref[0:feats, at] = high
        lhs_ref[feats : 2 * feats, at] = high
        lhs_ref[2 * feats : 3 * feats, at] = low
        lhs_ref[3 * feats :, at] = low
        for which in range(2):
            rvec_ref[which : which + 1, at] = pots[which]

    prepared = []
    for kind, first, last in ((0, 0, src_slabs), (1, src_slabs, slabs)):
        of_kind = [(col, slab) for col in range(num_cols) for slab in range(first, last)]
        for begin in range(0, len(of_kind), 2):
            members = of_kind[begin : begin + 2]
            trans, values, vecs = [], [], []
            for col, slab in members:
                value, pots = cell_terms(cols[col], slab)
                high, low = split(value)
                mid, least = split(low)
                both = jnp.concatenate([high, low], 0).T.astype(bf16)
                trans.append(jnp.concatenate([both, both], 1))
                stack = jnp.concatenate([high, mid, least, jnp.ones((16, LANES), f32)], 0)
                values.append(stack.astype(bf16))
                vecs.append(jnp.concatenate(pots + [jnp.zeros((6, LANES), f32)], 0).T)
            value = jnp.concatenate(values, 1)
            value = jnp.concatenate([value, value], 1)
            prepared.append((kind, members, jnp.concatenate(trans, 0), value, jnp.concatenate(vecs, 0)))

    begin = 0
    while begin < len(row_slabs):
        row_kind = 0 if begin * LANES < src_width else 1
        tile = row_slabs[begin : begin + 2]
        at = slice(begin * LANES, (begin + len(tile)) * LANES)
        begin += len(tile)
        sums = [None, None]
        for kind, members, trans, value, vecs in prepared:
            which = 1 if kind == row_kind else 0
            power = jnp.dot(trans, lhs_ref[:, at], preferred_element_type=f32)
            power = power + (rvec_ref[which : which + 1, at] + vecs[:, which : which + 1])
            weight = jnp.exp2(power)
            if own and kind == row_kind:
                for down, member in enumerate(members):
                    for across, other in enumerate(tile):
                        if member == other and member[0] == 0:
                            row_id = lax.broadcasted_iota(jnp.int32, weight.shape, 0) - down * LANES
                            col_id = lax.broadcasted_iota(jnp.int32, weight.shape, 1) - across * LANES
                            same = (row_id == col_id) & (row_id >= 0) & (row_id < LANES)
                            weight = jnp.where(same, 0.0, weight)
            high, low = split(weight)
            both = jnp.concatenate([high.astype(bf16), low.astype(bf16)], 0)
            part = jnp.dot(value, both, preferred_element_type=f32)
            sums[kind] = part if sums[kind] is None else sums[kind] + part
        sign = 1.0 if row_kind == 0 else -1.0
        total = sums[1] * (sign / totals[1]) - sums[0] * (sign / totals[0])
        mixed = total[0:feats] + total[feats : 2 * feats] + total[2 * feats : 3 * feats]
        mass = total[3 * feats : 3 * feats + 1]
        for across, (row, slab) in enumerate(tile):
            piece = slice(across * LANES, (across + 1) * LANES)
            value = rows[row][slab * feats : (slab + 1) * feats, :]
            grad = value * mass[:, piece] - mixed[:, piece]
            spot = slice(slab * LANES, (slab + 1) * LANES)
            if prev:
                grad = grad + prev[row][:, spot]
            outs[row][:, spot] = grad


def pair_terms(rows, cols, prev, own, shape, totals, cost=0):
    feats, src_slabs, tgt_slabs = shape
    width = (src_slabs + tgt_slabs) * LANES
    vmem = pl.BlockSpec(memory_space=pltpu.VMEM)
    args = [*rows, *cols, *prev]
    pairs = len(rows) * len(cols) * width**2
    return pl.pallas_call(
        functools.partial(pair_kernel, shape, len(rows), len(cols), own, totals),
        out_shape=[jax.ShapeDtypeStruct((feats, width), f32)] * len(rows),
        in_specs=[vmem] * len(args),
        out_specs=[vmem] * len(rows),
        scratch_shapes=[
            pltpu.VMEM((4 * feats, len(rows) * width), bf16),
            pltpu.VMEM((8, len(rows) * width), f32),
        ],
        compiler_params=pltpu.CompilerParams(vmem_limit_bytes=32 * 2**20),
        cost_estimate=pl.CostEstimate(flops=cost, bytes_accessed=2**20, transcendentals=0),
    )(*args)


def finish_kernel(mine_ref, near_ref, far_ref, src_ref, tgt_ref):
    count = src_ref.shape[1]
    src_ref[...] = mine_ref[:, :count] + near_ref[:, :count] + far_ref[:, :count]
    tgt_ref[...] = mine_ref[:, count:] + near_ref[:, count:] + far_ref[:, count:]


def body(src_latent, src_potential, tgt_latent, tgt_potential):
    feats, src_count = src_latent.shape
    tgt_count = tgt_latent.shape[1]
    src_slabs, tgt_slabs = src_count // LANES, tgt_count // LANES
    shape = (feats, src_slabs, tgt_slabs)
    slabs = src_slabs + tgt_slabs
    devices = lax.axis_size("src")
    totals = (src_count * devices, tgt_count * devices)
    pot_rows = -(-2 * slabs // 8) * 8
    vmem = pl.BlockSpec(memory_space=pltpu.VMEM)
    packed = pl.pallas_call(
        functools.partial(pack_kernel, slabs, feats),
        out_shape=jax.ShapeDtypeStruct((slabs * feats + pot_rows, LANES), f32),
        in_specs=[vmem] * 4,
        out_specs=vmem,
    )(src_latent, src_potential, tgt_latent, tgt_potential)

    def swap(value, bits):
        return lax.ppermute(value, "src", [(i, i ^ bits) for i in range(devices)])

    def terms(rows, cols, prev, own=False, cost=0):
        return pair_terms(rows, cols, prev, own, shape, totals, cost)

    across = swap(packed, 2)
    beside = swap(packed, 1)
    from_z = {k: swap(packed, k) for k in range(4, devices, 4)}
    rows = [packed, beside, across, swap(across, 1)]
    arrival = sorted(from_z, key=lambda k: (k % 8 == 0, -k))
    partial = terms(rows[:2], [packed], (), True, 10**10) + terms(rows[2:], [packed], ())
    partial = terms(rows, [from_z[arrival[0]]], partial)
    for k in arrival[1:-1]:
        partial = terms(rows, [from_z[k]], partial)
    last = from_z[arrival[-1]]
    to_across, to_corner = terms(rows[2:], [last], partial[2:])
    corner = swap(to_corner, 1)
    mine, to_beside = terms(rows[:2], [last], partial[:2])
    far = swap(to_across + corner, 2)
    near = swap(to_beside, 1)
    return pl.pallas_call(
        finish_kernel,
        out_shape=[jax.ShapeDtypeStruct(src_latent.shape, f32), jax.ShapeDtypeStruct(tgt_latent.shape, f32)],
        in_specs=[vmem] * 3,
        out_specs=[vmem] * 2,
        compiler_params=pltpu.CompilerParams(vmem_limit_bytes=4 * 2**20),
    )(mine, near, far)


def solution(mesh):
    spec = P(None, ("groups", "src"))
    return jax.shard_map(body, mesh=mesh, in_specs=(spec,) * 4, out_specs=(spec, spec), check_vma=False)
```

```python
import functools
import math

import jax
import jax.numpy as jnp
from jax import lax
from jax.experimental import pallas as pl
from jax.experimental.pallas import tpu as pltpu
from jax.sharding import PartitionSpec as P

SCALE = math.log2(math.e) / 0.1
LANES = 128
f32 = jnp.float32
bf16 = jnp.bfloat16


def split(value):
    high = value.astype(bf16).astype(f32)
    return high, value - high


def pack_kernel(slabs, feats, src_ref, srcp_ref, tgt_ref, tgtp_ref, out_ref):
    src_slabs = src_ref.shape[1] // LANES
    out_ref[slabs * feats :, :] = jnp.zeros((out_ref.shape[0] - slabs * feats, LANES), f32)
    for slab in range(slabs):
        ref, pot, at = (src_ref, srcp_ref, slab) if slab < src_slabs else (tgt_ref, tgtp_ref, slab - src_slabs)
        cols = slice(at * LANES, (at + 1) * LANES)
        out_ref[slab * feats : (slab + 1) * feats, :] = ref[:, cols]
        for which in range(2):
            row = slabs * feats + which * slabs + slab
            out_ref[row : row + 1, :] = pot[which : which + 1, cols]


def pair_kernel(shape, num_rows, num_cols, jobs, totals, prev_rows, joined, *refs):
    feats, src_slabs, tgt_slabs = shape
    slabs = src_slabs + tgt_slabs
    rows, cols = refs[:num_rows], refs[num_rows : num_rows + num_cols]
    num_outs = 1 if joined else num_rows
    prev = refs[num_rows + num_cols : -num_outs - 2]
    outs, lhs_ref, rvec_ref = refs[-num_outs - 2 : -2], refs[-2], refs[-1]
    if joined:
        width = slabs * LANES
        outs = [outs[0].at[:, row * width : (row + 1) * width] for row in range(num_rows)]
    sums_so_far = dict(zip(prev_rows, prev))

    def cell_terms(ref, slab):
        value = ref[slab * feats : (slab + 1) * feats, :]
        norm = 0.5 * jnp.sum(value * value, 0, keepdims=True)
        first = slabs * feats + slab
        pots = [SCALE * (ref[first + which * slabs : first + which * slabs + 1, :] - norm) for which in range(2)]
        return value, pots

    row_slabs = [(row, slab) for row in range(num_rows) for slab in range(src_slabs)]
    row_slabs += [(row, slab) for row in range(num_rows) for slab in range(src_slabs, slabs)]
    for place, (row, slab) in enumerate(row_slabs):
        value, pots = cell_terms(rows[row], slab)
        high, low = split(value * SCALE)
        high, low = high.astype(bf16), low.astype(bf16)
        at = slice(place * LANES, (place + 1) * LANES)
        lhs_ref[0:feats, at] = high
        lhs_ref[feats : 2 * feats, at] = high
        lhs_ref[2 * feats : 3 * feats, at] = low
        lhs_ref[3 * feats :, at] = low
        for which in range(2):
            rvec_ref[which : which + 1, at] = pots[which]

    @functools.cache
    def prepare(members):
        trans, values, vecs = [], [], []
        for col, slab in members:
            value, pots = cell_terms(cols[col], slab)
            high, low = split(value)
            mid, least = split(low)
            both = jnp.concatenate([high, low], 0).T.astype(bf16)
            trans.append(jnp.concatenate([both, both], 1))
            stack = jnp.concatenate([high, mid, least, jnp.ones((16, LANES), f32)], 0)
            values.append(stack.astype(bf16))
            vecs.append(jnp.concatenate(pots + [jnp.zeros((6, LANES), f32)], 0).T)
        value = jnp.concatenate(values, 1)
        return jnp.concatenate(trans, 0), jnp.concatenate([value, value], 1), jnp.concatenate(vecs, 0)

    def run_tile(tile, prepared, own):
        row_kind = 0 if tile[0][1] < src_slabs else 1
        place = row_slabs.index(tile[0])
        at = slice(place * LANES, (place + len(tile)) * LANES)
        sums = [None, None]
        for kind, members, (trans, value, vecs) in prepared:
            which = 1 if kind == row_kind else 0
            power = jnp.dot(trans, lhs_ref[:, at], preferred_element_type=f32)
            power = power + (rvec_ref[which : which + 1, at] + vecs[:, which : which + 1])
            weight = jnp.exp2(power)
            if own and kind == row_kind:
                for down, member in enumerate(members):
                    for across, other in enumerate(tile):
                        if member == other:
                            row_id = lax.broadcasted_iota(jnp.int32, weight.shape, 0) - down * LANES
                            col_id = lax.broadcasted_iota(jnp.int32, weight.shape, 1) - across * LANES
                            same = (row_id == col_id) & (row_id >= 0) & (row_id < LANES)
                            weight = jnp.where(same, 0.0, weight)
            high, low = split(weight)
            both = jnp.concatenate([high.astype(bf16), low.astype(bf16)], 0)
            part = jnp.dot(value, both, preferred_element_type=f32)
            sums[kind] = part if sums[kind] is None else sums[kind] + part
        sign = 1.0 if row_kind == 0 else -1.0
        total = sums[1] * (sign / totals[1]) - sums[0] * (sign / totals[0])
        mixed = total[0:feats] + total[feats : 2 * feats] + total[2 * feats : 3 * feats]
        mass = total[3 * feats : 3 * feats + 1]
        for across, (row, slab) in enumerate(tile):
            piece = slice(across * LANES, (across + 1) * LANES)
            value = rows[row][slab * feats : (slab + 1) * feats, :]
            grad = value * mass[:, piece] - mixed[:, piece]
            spot = slice(slab * LANES, (slab + 1) * LANES)
            if row in sums_so_far:
                grad = grad + sums_so_far[row][:, spot]
            outs[row][:, spot] = grad

    for job_rows, job_cols, own in jobs:
        prepared = []
        for kind, first, last in ((0, 0, src_slabs), (1, src_slabs, slabs)):
            of_kind = [(col, slab) for col in job_cols for slab in range(first, last)]
            for begin in range(0, len(of_kind), 2):
                members = of_kind[begin : begin + 2]
                prepared.append((kind, members, prepare(tuple(members))))
        for first, last in ((0, src_slabs), (src_slabs, slabs)):
            of_kind = [(row, slab) for row in job_rows for slab in range(first, last)]
            for begin in range(0, len(of_kind), 2):
                run_tile(of_kind[begin : begin + 2], prepared, own)
        for row in job_rows:
            sums_so_far[row] = outs[row]


def pair_terms(shape, totals, rows, cols, prev, jobs, cost=0, joined=False):
    feats, src_slabs, tgt_slabs = shape
    width = (src_slabs + tgt_slabs) * LANES
    vmem = pl.BlockSpec(memory_space=pltpu.VMEM)
    one = jax.ShapeDtypeStruct((feats, width), f32)
    prev_rows = [row for row, value in enumerate(prev) if value is not None]
    args = [*rows, *cols, *[prev[row] for row in prev_rows]]
    return pl.pallas_call(
        functools.partial(pair_kernel, shape, len(rows), len(cols), jobs, totals, prev_rows, joined),
        out_shape=jax.ShapeDtypeStruct((feats, len(rows) * width), f32) if joined else [one] * len(rows),
        in_specs=[vmem] * len(args),
        out_specs=vmem if joined else [vmem] * len(rows),
        scratch_shapes=[
            pltpu.VMEM((4 * feats, len(rows) * width), bf16),
            pltpu.VMEM((8, len(rows) * width), f32),
        ],
        compiler_params=pltpu.CompilerParams(vmem_limit_bytes=32 * 2**20),
        cost_estimate=pl.CostEstimate(flops=cost, bytes_accessed=2**20, transcendentals=0),
    )(*args)


def finish_kernel(mine_ref, near_ref, src_ref, tgt_ref):
    count = src_ref.shape[1]
    src_ref[...] = mine_ref[:, :count] + near_ref[:, :count]
    tgt_ref[...] = mine_ref[:, count:] + near_ref[:, count:]


def body(src_latent, src_potential, tgt_latent, tgt_potential):
    feats, src_count = src_latent.shape
    tgt_count = tgt_latent.shape[1]
    src_slabs, tgt_slabs = src_count // LANES, tgt_count // LANES
    shape = (feats, src_slabs, tgt_slabs)
    slabs = src_slabs + tgt_slabs
    devices = lax.axis_size("src")
    totals = (src_count * devices, tgt_count * devices)
    pot_rows = -(-2 * slabs // 8) * 8
    vmem = pl.BlockSpec(memory_space=pltpu.VMEM)
    packed = pl.pallas_call(
        functools.partial(pack_kernel, slabs, feats),
        out_shape=jax.ShapeDtypeStruct((slabs * feats + pot_rows, LANES), f32),
        in_specs=[vmem] * 4,
        out_specs=vmem,
    )(src_latent, src_potential, tgt_latent, tgt_potential)

    def swap(value, bits):
        return lax.ppermute(value, "src", [(i, i ^ bits) for i in range(devices)])

    terms = functools.partial(pair_terms, shape, totals)
    across = swap(packed, 2)
    beside = swap(packed, 1)
    from_z = {k: swap(packed, k) for k in range(4, devices, 4)}
    arrival = sorted(from_z, key=lambda k: (k % 8 == 0, -k))
    early, middle, last = from_z[arrival[0]], arrival[1:-1], from_z[arrival[-1]]
    near_z = from_z[middle[-1]]
    (mine,) = terms([packed], [packed], [None], [((0,), (0,), True)], 0)
    (mine,) = terms([packed], [early], [mine], [((0,), (0,), False)])
    mine, later, beside = lax.optimization_barrier((mine, across, beside))
    corner = swap(later, 1)
    near, wide = terms([beside, later], [packed, early], [None] * 2, [((0, 1), (0, 1), False)], 10000000000)
    corner, wide = lax.optimization_barrier((corner, wide))
    (sent,) = terms([corner], [packed, early], [None], [((0,), (0, 1), False)], 0)
    wide, sent = terms([across, corner], [near_z], [wide, sent], [((0, 1), (0,), False)])
    for at in range(0, len(middle) - 1, 2):
        group = [from_z[k] for k in middle[at : min(at + 2, len(middle) - 1)]]
        jobs = [((0, 1, 2, 3), tuple(range(len(group))), False)]
        mine, near, wide, sent = terms([packed, beside, across, corner], group, [mine, near, wide, sent], jobs)
    (sent,) = terms([corner], [last], [sent], [((0,), (0,), False)])
    got = swap(sent, 1)
    (wide,) = terms([across], [last], [wide], [((0,), (0,), False)])
    send = wide + got
    far = swap(send, 2)
    last, send = lax.optimization_barrier((last, send))
    mine, near = terms([packed, beside], [near_z, last], [mine, near], [((0, 1), (0, 1), False)])
    near = swap(near, 1)
    mine = mine + far
    return pl.pallas_call(
        finish_kernel,
        out_shape=[jax.ShapeDtypeStruct(src_latent.shape, f32), jax.ShapeDtypeStruct(tgt_latent.shape, f32)],
        in_specs=[vmem] * 2,
        out_specs=[vmem] * 2,
        compiler_params=pltpu.CompilerParams(vmem_limit_bytes=4 * 2**20),
    )(mine, near)


def solution(mesh):
    spec = P(None, ("groups", "src"))
    return jax.shard_map(body, mesh=mesh, in_specs=(spec,) * 4, out_specs=(spec, spec), check_vma=False)
```

```python
import functools
import math

import jax
import jax.numpy as jnp
from jax import lax
from jax.experimental import pallas as pl
from jax.experimental.pallas import tpu as pltpu
from jax.sharding import PartitionSpec as P

SCALE = math.log2(math.e) / 0.1
LANES = 128
f32 = jnp.float32
bf16 = jnp.bfloat16


def split(value):
    high = value.astype(bf16).astype(f32)
    return high, value - high


def pack_kernel(slabs, feats, src_ref, srcp_ref, tgt_ref, tgtp_ref, out_ref, srcp_held, tgtp_held, sems):
    src_slabs = src_ref.shape[1] // LANES
    held = (srcp_held, tgtp_held)
    copies = [pltpu.make_async_copy(ref, to, sems.at[at]) for at, (ref, to) in enumerate(zip((srcp_ref, tgtp_ref), held))]
    for slab in range(slabs):
        ref, at = (src_ref, slab) if slab < src_slabs else (tgt_ref, slab - src_slabs)
        to = out_ref.at[slab * feats : (slab + 1) * feats, :]
        copies.append(pltpu.make_async_copy(ref.at[:, at * LANES : (at + 1) * LANES], to, sems.at[2 + slab]))
    for copy in copies:
        copy.start()
    out_ref[slabs * feats :, :] = jnp.zeros((out_ref.shape[0] - slabs * feats, LANES), f32)
    for copy in copies[:2]:
        copy.wait()
    for slab in range(slabs):
        pot, at = (srcp_held, slab) if slab < src_slabs else (tgtp_held, slab - src_slabs)
        for which in range(2):
            row = slabs * feats + which * slabs + slab
            out_ref[row : row + 1, :] = pot[which : which + 1, at * LANES : (at + 1) * LANES]
    for copy in copies[2:]:
        copy.wait()


def pair_kernel(shape, num_rows, num_cols, jobs, totals, prev_rows, joined, *refs):
    feats, src_slabs, tgt_slabs = shape
    slabs = src_slabs + tgt_slabs
    rows, cols = refs[:num_rows], refs[num_rows : num_rows + num_cols]
    num_outs = 1 if joined else num_rows
    prev = refs[num_rows + num_cols : -num_outs - 2]
    outs, lhs_ref, rvec_ref = refs[-num_outs - 2 : -2], refs[-2], refs[-1]
    if joined:
        width = slabs * LANES
        outs = [outs[0].at[:, row * width : (row + 1) * width] for row in range(num_rows)]
    sums_so_far = dict(zip(prev_rows, prev))

    def cell_terms(ref, slab):
        value = ref[slab * feats : (slab + 1) * feats, :]
        norm = 0.5 * jnp.sum(value * value, 0, keepdims=True)
        first = slabs * feats + slab
        pots = [SCALE * (ref[first + which * slabs : first + which * slabs + 1, :] - norm) for which in range(2)]
        return value, pots

    row_slabs = [(row, slab) for row in range(num_rows) for slab in range(src_slabs)]
    row_slabs += [(row, slab) for row in range(num_rows) for slab in range(src_slabs, slabs)]
    for place, (row, slab) in enumerate(row_slabs):
        value, pots = cell_terms(rows[row], slab)
        high, low = split(value * SCALE)
        high, low = high.astype(bf16), low.astype(bf16)
        at = slice(place * LANES, (place + 1) * LANES)
        lhs_ref[0:feats, at] = high
        lhs_ref[feats : 2 * feats, at] = high
        lhs_ref[2 * feats : 3 * feats, at] = low
        lhs_ref[3 * feats :, at] = low
        for which in range(2):
            rvec_ref[which : which + 1, at] = pots[which]

    @functools.cache
    def prepare(members):
        trans, values, vecs = [], [], []
        for col, slab in members:
            value, pots = cell_terms(cols[col], slab)
            high, low = split(value)
            mid, least = split(low)
            both = jnp.concatenate([high, low], 0).T.astype(bf16)
            trans.append(jnp.concatenate([both, both], 1))
            stack = jnp.concatenate([high, mid, least, jnp.ones((16, LANES), f32)], 0)
            values.append(stack.astype(bf16))
            vecs.append(jnp.concatenate(pots + [jnp.zeros((6, LANES), f32)], 0).T)
        value = jnp.concatenate(values, 1)
        return jnp.concatenate(trans, 0), jnp.concatenate([value, value], 1), jnp.concatenate(vecs, 0)

    def run_tile(tile, prepared, own):
        row_kind = 0 if tile[0][1] < src_slabs else 1
        place = row_slabs.index(tile[0])
        at = slice(place * LANES, (place + len(tile)) * LANES)
        sums = [None, None]
        for kind, members, (trans, value, vecs) in prepared:
            which = 1 if kind == row_kind else 0
            power = jnp.dot(trans, lhs_ref[:, at], preferred_element_type=f32)
            power = power + (rvec_ref[which : which + 1, at] + vecs[:, which : which + 1])
            weight = jnp.exp2(power)
            if own and kind == row_kind:
                for down, member in enumerate(members):
                    for across, other in enumerate(tile):
                        if member == other:
                            row_id = lax.broadcasted_iota(jnp.int32, weight.shape, 0) - down * LANES
                            col_id = lax.broadcasted_iota(jnp.int32, weight.shape, 1) - across * LANES
                            same = (row_id == col_id) & (row_id >= 0) & (row_id < LANES)
                            weight = jnp.where(same, 0.0, weight)
            high, low = split(weight)
            both = jnp.concatenate([high.astype(bf16), low.astype(bf16)], 0)
            part = jnp.dot(value, both, preferred_element_type=f32)
            sums[kind] = part if sums[kind] is None else sums[kind] + part
        sign = 1.0 if row_kind == 0 else -1.0
        total = sums[1] * (sign / totals[1]) - sums[0] * (sign / totals[0])
        mixed = total[0:feats] + total[feats : 2 * feats] + total[2 * feats : 3 * feats]
        mass = total[3 * feats : 3 * feats + 1]
        for across, (row, slab) in enumerate(tile):
            piece = slice(across * LANES, (across + 1) * LANES)
            value = rows[row][slab * feats : (slab + 1) * feats, :]
            grad = value * mass[:, piece] - mixed[:, piece]
            spot = slice(slab * LANES, (slab + 1) * LANES)
            if row in sums_so_far:
                grad = grad + sums_so_far[row][:, spot]
            outs[row][:, spot] = grad

    for job_rows, job_cols, own in jobs:
        prepared = []
        for kind, first, last in ((0, 0, src_slabs), (1, src_slabs, slabs)):
            of_kind = [(col, slab) for col in job_cols for slab in range(first, last)]
            for begin in range(0, len(of_kind), 2):
                members = of_kind[begin : begin + 2]
                prepared.append((kind, members, prepare(tuple(members))))
        for first, last in ((0, src_slabs), (src_slabs, slabs)):
            of_kind = [(row, slab) for row in job_rows for slab in range(first, last)]
            for begin in range(0, len(of_kind), 2):
                run_tile(of_kind[begin : begin + 2], prepared, own)
        for row in job_rows:
            sums_so_far[row] = outs[row]


def pair_terms(shape, totals, rows, cols, prev, jobs, cost=0, joined=False):
    feats, src_slabs, tgt_slabs = shape
    width = (src_slabs + tgt_slabs) * LANES
    vmem = pl.BlockSpec(memory_space=pltpu.VMEM)
    one = jax.ShapeDtypeStruct((feats, width), f32)
    prev_rows = [row for row, value in enumerate(prev) if value is not None]
    args = [*rows, *cols, *[prev[row] for row in prev_rows]]
    return pl.pallas_call(
        functools.partial(pair_kernel, shape, len(rows), len(cols), jobs, totals, prev_rows, joined),
        out_shape=jax.ShapeDtypeStruct((feats, len(rows) * width), f32) if joined else [one] * len(rows),
        in_specs=[vmem] * len(args),
        out_specs=vmem if joined else [vmem] * len(rows),
        scratch_shapes=[
            pltpu.VMEM((4 * feats, len(rows) * width), bf16),
            pltpu.VMEM((8, len(rows) * width), f32),
        ],
        compiler_params=pltpu.CompilerParams(vmem_limit_bytes=32 * 2**20),
        cost_estimate=pl.CostEstimate(flops=cost, bytes_accessed=2**20, transcendentals=0),
    )(*args)


def finish_kernel(mine_ref, near_ref, src_ref, tgt_ref):
    count = src_ref.shape[1]
    src_ref[...] = mine_ref[:, :count] + near_ref[:, :count]
    tgt_ref[...] = mine_ref[:, count:] + near_ref[:, count:]


def body(src_latent, src_potential, tgt_latent, tgt_potential):
    feats, src_count = src_latent.shape
    tgt_count = tgt_latent.shape[1]
    src_slabs, tgt_slabs = src_count // LANES, tgt_count // LANES
    shape = (feats, src_slabs, tgt_slabs)
    slabs = src_slabs + tgt_slabs
    devices = lax.axis_size("src")
    totals = (src_count * devices, tgt_count * devices)
    pot_rows = -(-2 * slabs // 8) * 8
    vmem = pl.BlockSpec(memory_space=pltpu.VMEM)
    hbm = pl.BlockSpec(memory_space=pltpu.HBM)
    args = (src_latent, src_potential, tgt_latent, tgt_potential)
    packed = pl.pallas_call(
        functools.partial(pack_kernel, slabs, feats),
        out_shape=pltpu.VMEM((slabs * feats + pot_rows, LANES), f32),
        in_specs=[hbm] * 4,
        out_specs=vmem,
        scratch_shapes=[
            pltpu.VMEM(src_potential.shape, f32),
            pltpu.VMEM(tgt_potential.shape, f32),
            pltpu.SemaphoreType.DMA((2 + slabs,)),
        ],
        compiler_params=pltpu.CompilerParams(vmem_limit_bytes=4 * 2**20),
    )(*[pltpu.with_memory_space_constraint(arg, pltpu.HBM) for arg in args])

    def swap(value, bits):
        return lax.ppermute(value, "src", [(i, i ^ bits) for i in range(devices)])

    terms = functools.partial(pair_terms, shape, totals)
    across = swap(packed, 2)
    beside = swap(packed, 1)
    from_z = {k: swap(packed, k) for k in range(4, devices, 4)}
    arrival = sorted(from_z, key=lambda k: (k % 8 == 0, -k))
    early, middle, last = from_z[arrival[0]], arrival[1:-1], from_z[arrival[-1]]
    near_z = from_z[middle[-1]]
    (mine,) = terms([packed], [packed], [None], [((0,), (0,), True)], 0)
    (mine,) = terms([packed], [early], [mine], [((0,), (0,), False)])
    mine, later, beside = lax.optimization_barrier((mine, across, beside))
    corner = swap(later, 1)
    near, wide = terms([beside, later], [packed, early], [None] * 2, [((0, 1), (0, 1), False)], 10000000000)
    corner, wide = lax.optimization_barrier((corner, wide))
    (sent,) = terms([corner], [packed, early], [None], [((0,), (0, 1), False)], 0)
    wide, sent = terms([across, corner], [near_z], [wide, sent], [((0, 1), (0,), False)])
    for at in range(0, len(middle) - 1, 2):
        group = [from_z[k] for k in middle[at : min(at + 2, len(middle) - 1)]]
        jobs = [((0, 1, 2, 3), tuple(range(len(group))), False)]
        mine, near, wide, sent = terms([packed, beside, across, corner], group, [mine, near, wide, sent], jobs)
    (sent,) = terms([corner], [last], [sent], [((0,), (0,), False)])
    got = swap(sent, 1)
    (wide,) = terms([across], [last], [wide], [((0,), (0,), False)])
    send = wide + got
    far = swap(send, 2)
    last, send = lax.optimization_barrier((last, send))
    mine, near = terms([packed, beside], [near_z, last], [mine, near], [((0, 1), (0, 1), False)])
    near = swap(near, 1)
    mine = mine + far
    return pl.pallas_call(
        finish_kernel,
        out_shape=[jax.ShapeDtypeStruct(src_latent.shape, f32), jax.ShapeDtypeStruct(tgt_latent.shape, f32)],
        in_specs=[vmem] * 2,
        out_specs=[vmem] * 2,
        compiler_params=pltpu.CompilerParams(vmem_limit_bytes=4 * 2**20),
    )(mine, near)


def solution(mesh):
    spec = P(None, ("groups", "src"))
    return jax.shard_map(body, mesh=mesh, in_specs=(spec,) * 4, out_specs=(spec, spec), check_vma=False)
```

```python
import functools
import math

import jax
import jax.numpy as jnp
from jax import lax
from jax.experimental import pallas as pl
from jax.experimental.pallas import tpu as pltpu
from jax.sharding import PartitionSpec as P

SCALE = math.log2(math.e) / 0.1
LANES = 128
f32 = jnp.float32
bf16 = jnp.bfloat16


def split(value):
    high = value.astype(bf16).astype(f32)
    return high, value - high


def pack_kernel(slabs, feats, src_ref, srcp_ref, tgt_ref, tgtp_ref, out_ref, srcp_held, tgtp_held, sems):
    src_slabs = src_ref.shape[1] // LANES
    held = (srcp_held, tgtp_held)
    copies = [pltpu.make_async_copy(ref, to, sems.at[at]) for at, (ref, to) in enumerate(zip((srcp_ref, tgtp_ref), held))]
    for slab in range(slabs):
        ref, at = (src_ref, slab) if slab < src_slabs else (tgt_ref, slab - src_slabs)
        to = out_ref.at[slab * feats : (slab + 1) * feats, :]
        copies.append(pltpu.make_async_copy(ref.at[:, at * LANES : (at + 1) * LANES], to, sems.at[2 + slab]))
    for copy in copies:
        copy.start()
    out_ref[slabs * feats :, :] = jnp.zeros((out_ref.shape[0] - slabs * feats, LANES), f32)
    for copy in copies[:2]:
        copy.wait()
    for slab in range(slabs):
        pot, at = (srcp_held, slab) if slab < src_slabs else (tgtp_held, slab - src_slabs)
        for which in range(2):
            row = slabs * feats + which * slabs + slab
            out_ref[row : row + 1, :] = pot[which : which + 1, at * LANES : (at + 1) * LANES]
    for copy in copies[2:]:
        copy.wait()


def cell_terms(shape, ref, slab):
    feats, src_slabs, tgt_slabs = shape
    slabs = src_slabs + tgt_slabs
    value = ref[slab * feats : (slab + 1) * feats, :]
    norm = 0.5 * jnp.sum(value * value, 0, keepdims=True)
    first = slabs * feats + slab
    pots = [SCALE * (ref[first + which * slabs : first + which * slabs + 1, :] - norm) for which in range(2)]
    return value, pots


def store_row(shape, ref, lhs_ref, vec_ref):
    feats, src_slabs, tgt_slabs = shape
    for slab in range(src_slabs + tgt_slabs):
        value, pots = cell_terms(shape, ref, slab)
        high, low = split(value * SCALE)
        both = jnp.concatenate([high, low], 0).T.astype(bf16)
        at = slice(slab * LANES, (slab + 1) * LANES)
        lhs_ref[at, 0:LANES] = both
        lhs_ref[at, LANES:] = both
        for which in range(2):
            vec_ref[which, at, :] = jnp.broadcast_to(pots[which], (LANES, LANES)).T


def pair_kernel(shape, num_rows, num_cols, jobs, totals, prev_rows, keep, *refs):
    feats, src_slabs, tgt_slabs = shape
    slabs = src_slabs + tgt_slabs
    rows, cols = refs[:num_rows], refs[num_rows : num_rows + num_cols]
    lhs_ref, rvec_ref = refs[-2:]
    refs = refs[num_rows + num_cols : -2]
    prev, refs = refs[: len(prev_rows)], refs[len(prev_rows) :]
    outs = refs[:num_rows]
    if keep is not None:
        store_row(shape, rows[keep], *refs[num_rows:])
    sums_so_far = dict(zip(prev_rows, prev))

    row_slabs = [(row, slab) for row in range(num_rows) for slab in range(src_slabs)]
    row_slabs += [(row, slab) for row in range(num_rows) for slab in range(src_slabs, slabs)]
    for place, (row, slab) in enumerate(row_slabs):
        value, pots = cell_terms(shape, rows[row], slab)
        high, low = split(value * SCALE)
        high, low = high.astype(bf16), low.astype(bf16)
        at = slice(place * LANES, (place + 1) * LANES)
        lhs_ref[0:feats, at] = high
        lhs_ref[feats : 2 * feats, at] = high
        lhs_ref[2 * feats : 3 * feats, at] = low
        lhs_ref[3 * feats :, at] = low
        for which in range(2):
            rvec_ref[which : which + 1, at] = pots[which]

    @functools.cache
    def prepare(members):
        trans, values, vecs = [], [], []
        for col, slab in members:
            value, pots = cell_terms(shape, cols[col], slab)
            high, low = split(value)
            mid, least = split(low)
            both = jnp.concatenate([high, low], 0).T.astype(bf16)
            trans.append(jnp.concatenate([both, both], 1))
            stack = jnp.concatenate([high, mid, least, jnp.ones((16, LANES), f32)], 0)
            values.append(stack.astype(bf16))
            vecs.append(jnp.concatenate(pots + [jnp.zeros((6, LANES), f32)], 0).T)
        value = jnp.concatenate(values, 1)
        return jnp.concatenate(trans, 0), jnp.concatenate([value, value], 1), jnp.concatenate(vecs, 0)

    def run_tile(tile, prepared, own):
        row_kind = 0 if tile[0][1] < src_slabs else 1
        place = row_slabs.index(tile[0])
        at = slice(place * LANES, (place + len(tile)) * LANES)
        sums = [None, None]
        for kind, members, (trans, value, vecs) in prepared:
            which = 1 if kind == row_kind else 0
            power = jnp.dot(trans, lhs_ref[:, at], preferred_element_type=f32)
            power = power + (rvec_ref[which : which + 1, at] + vecs[:, which : which + 1])
            weight = jnp.exp2(power)
            if own and kind == row_kind:
                for down, member in enumerate(members):
                    for across, other in enumerate(tile):
                        if member == other:
                            row_id = lax.broadcasted_iota(jnp.int32, weight.shape, 0) - down * LANES
                            col_id = lax.broadcasted_iota(jnp.int32, weight.shape, 1) - across * LANES
                            same = (row_id == col_id) & (row_id >= 0) & (row_id < LANES)
                            weight = jnp.where(same, 0.0, weight)
            high, low = split(weight)
            both = jnp.concatenate([high.astype(bf16), low.astype(bf16)], 0)
            part = jnp.dot(value, both, preferred_element_type=f32)
            sums[kind] = part if sums[kind] is None else sums[kind] + part
        sign = 1.0 if row_kind == 0 else -1.0
        total = sums[1] * (sign / totals[1]) - sums[0] * (sign / totals[0])
        mixed = total[0:feats] + total[feats : 2 * feats] + total[2 * feats : 3 * feats]
        mass = total[3 * feats : 3 * feats + 1]
        for across, (row, slab) in enumerate(tile):
            piece = slice(across * LANES, (across + 1) * LANES)
            value = rows[row][slab * feats : (slab + 1) * feats, :]
            grad = value * mass[:, piece] - mixed[:, piece]
            spot = slice(slab * LANES, (slab + 1) * LANES)
            if row in sums_so_far:
                grad = grad + sums_so_far[row][:, spot]
            outs[row][:, spot] = grad

    for job_rows, job_cols, own in jobs:
        prepared = []
        for kind, first, last in ((0, 0, src_slabs), (1, src_slabs, slabs)):
            of_kind = [(col, slab) for col in job_cols for slab in range(first, last)]
            for begin in range(0, len(of_kind), 2):
                members = of_kind[begin : begin + 2]
                prepared.append((kind, members, prepare(tuple(members))))
        for first, last in ((0, src_slabs), (src_slabs, slabs)):
            of_kind = [(row, slab) for row in job_rows for slab in range(first, last)]
            for begin in range(0, len(of_kind), 2):
                run_tile(of_kind[begin : begin + 2], prepared, own)
        for row in job_rows:
            sums_so_far[row] = outs[row]


def pair_terms(shape, totals, rows, cols, prev, jobs, cost=0, keep=None):
    feats, src_slabs, tgt_slabs = shape
    width = (src_slabs + tgt_slabs) * LANES
    vmem = pl.BlockSpec(memory_space=pltpu.VMEM)
    prev_rows = [row for row, value in enumerate(prev) if value is not None]
    args = [*rows, *cols, *[prev[row] for row in prev_rows]]
    outs = [jax.ShapeDtypeStruct((feats, width), f32)] * len(rows)
    if keep is not None:
        outs += [jax.ShapeDtypeStruct((width, 4 * feats), bf16), jax.ShapeDtypeStruct((2, width, LANES), f32)]
    return pl.pallas_call(
        functools.partial(pair_kernel, shape, len(rows), len(cols), jobs, totals, prev_rows, keep),
        out_shape=outs,
        in_specs=[vmem] * len(args),
        out_specs=[vmem] * len(outs),
        scratch_shapes=[
            pltpu.VMEM((4 * feats, len(rows) * width), bf16),
            pltpu.VMEM((8, len(rows) * width), f32),
        ],
        compiler_params=pltpu.CompilerParams(vmem_limit_bytes=32 * 2**20),
        cost_estimate=pl.CostEstimate(flops=cost, bytes_accessed=2**20, transcendentals=0),
    )(*args)


def late_kernel(shape, totals, block, lhs_ref, vec_ref, col, prev, out):
    feats, src_slabs, tgt_slabs = shape
    slabs = src_slabs + tgt_slabs
    kinds = []
    for first, last in ((0, src_slabs), (src_slabs, slabs)):
        natural, values, vecs = [], [], [[], []]
        for slab in range(first, last):
            value, pots = cell_terms(shape, col, slab)
            high, low = split(value)
            mid, least = split(low)
            high, low, mid, least = (part.astype(bf16) for part in (high, low, mid, least))
            natural.append(jnp.concatenate([high, high, low, low], 0))
            values.append(jnp.concatenate([high, mid, least, jnp.ones((16, LANES), bf16)], 0))
            for which in range(2):
                vecs[which].append(pots[which])
        value = jnp.concatenate(values, 1)
        value = jnp.concatenate([value, value], 1)
        kinds.append((jnp.concatenate(natural, 1), value, [jnp.concatenate(vec, 1) for vec in vecs]))

    for row_kind, (first, last) in enumerate(((0, src_slabs), (src_slabs, slabs))):
        at = slice(first * LANES, last * LANES)
        sums = []
        for kind, (natural, value, vecs) in enumerate(kinds):
            which = 1 if kind == row_kind else 0
            power = jnp.dot(lhs_ref[at, :], natural, preferred_element_type=f32)
            spread = jnp.concatenate([vec_ref[which, at, :]] * (natural.shape[1] // LANES), 1)
            weight = jnp.exp2(power + (spread + vecs[which]))
            high, low = split(weight)
            both = jnp.concatenate([high.astype(bf16), low.astype(bf16)], 1)
            sums.append(lax.dot_general(value, both, (((1,), (1,)), ((), ())), preferred_element_type=f32))
        sign = 1.0 if row_kind == 0 else -1.0
        total = sums[1] * (sign / totals[1]) - sums[0] * (sign / totals[0])
        mixed = total[0:feats] + total[feats : 2 * feats] + total[2 * feats : 3 * feats]
        mass = total[3 * feats : 3 * feats + 1]
        for slab in range(first, last):
            piece = slice((slab - first) * LANES, (slab - first + 1) * LANES)
            spot = slice(slab * LANES, (slab + 1) * LANES)
            value = block[slab * feats : (slab + 1) * feats, :]
            out[:, spot] = value * mass[:, piece] - mixed[:, piece] + prev[:, spot]


def late_terms(shape, totals, row, col, prev):
    vmem = pl.BlockSpec(memory_space=pltpu.VMEM)
    return pl.pallas_call(
        functools.partial(late_kernel, shape, totals),
        out_shape=jax.ShapeDtypeStruct(prev.shape, f32),
        in_specs=[vmem] * 5,
        out_specs=vmem,
        compiler_params=pltpu.CompilerParams(vmem_limit_bytes=32 * 2**20),
        cost_estimate=pl.CostEstimate(flops=0, bytes_accessed=2**20, transcendentals=0),
    )(*row, col, prev)


def finish_kernel(mine_ref, near_ref, src_ref, tgt_ref):
    count = src_ref.shape[1]
    src_ref[...] = mine_ref[:, :count] + near_ref[:, :count]
    tgt_ref[...] = mine_ref[:, count:] + near_ref[:, count:]


def body(src_latent, src_potential, tgt_latent, tgt_potential):
    feats, src_count = src_latent.shape
    tgt_count = tgt_latent.shape[1]
    src_slabs, tgt_slabs = src_count // LANES, tgt_count // LANES
    shape = (feats, src_slabs, tgt_slabs)
    slabs = src_slabs + tgt_slabs
    devices = lax.axis_size("src")
    totals = (src_count * devices, tgt_count * devices)
    pot_rows = -(-2 * slabs // 8) * 8
    vmem = pl.BlockSpec(memory_space=pltpu.VMEM)
    hbm = pl.BlockSpec(memory_space=pltpu.HBM)
    args = (src_latent, src_potential, tgt_latent, tgt_potential)
    packed = pl.pallas_call(
        functools.partial(pack_kernel, slabs, feats),
        out_shape=pltpu.VMEM((slabs * feats + pot_rows, LANES), f32),
        in_specs=[hbm] * 4,
        out_specs=vmem,
        scratch_shapes=[
            pltpu.VMEM(src_potential.shape, f32),
            pltpu.VMEM(tgt_potential.shape, f32),
            pltpu.SemaphoreType.DMA((2 + slabs,)),
        ],
        compiler_params=pltpu.CompilerParams(vmem_limit_bytes=4 * 2**20),
    )(*[pltpu.with_memory_space_constraint(arg, pltpu.HBM) for arg in args])

    def swap(value, bits):
        return lax.ppermute(value, "src", [(i, i ^ bits) for i in range(devices)])

    terms = functools.partial(pair_terms, shape, totals)
    across = swap(packed, 2)
    beside = swap(packed, 1)
    from_z = {k: swap(packed, k) for k in range(4, devices, 4)}
    arrival = sorted(from_z, key=lambda k: (k % 8 == 0, -k))
    early, middle, last = from_z[arrival[0]], arrival[1:-1], from_z[arrival[-1]]
    near_z = from_z[middle[-1]]
    (mine,) = terms([packed], [packed, early], [None], [((0,), (0, 1), True)])
    mine, later, beside = lax.optimization_barrier((mine, across, beside))
    corner = swap(later, 1)
    jobs = [((0, 1), (0, 1), False)]
    near, wide, *row_later = terms([beside, later], [packed, early], [None] * 2, jobs, 10**10, 1)
    corner, wide = lax.optimization_barrier((corner, wide))
    sent, *row_corner = terms([corner], [packed, early], [None], [((0,), (0, 1), False)], 0, 0)
    wide, sent = terms([across, corner], [near_z], [wide, sent], [((0, 1), (0,), False)])
    for at in range(0, len(middle) - 1, 2):
        group = [from_z[k] for k in middle[at : min(at + 2, len(middle) - 1)]]
        jobs = [((0, 1, 2, 3), tuple(range(len(group))), False)]
        mine, near, wide, sent = terms([packed, beside, across, corner], group, [mine, near, wide, sent], jobs)
    sent = late_terms(shape, totals, (corner, *row_corner), last, sent)
    got = swap(sent, 1)
    wide = late_terms(shape, totals, (across, *row_later), last, wide)
    send = wide + got
    far = swap(send, 2)
    last, send = lax.optimization_barrier((last, send))
    mine, near = terms([packed, beside], [near_z, last], [mine, near], [((0, 1), (0, 1), False)])
    near = swap(near, 1)
    mine = mine + far
    return pl.pallas_call(
        finish_kernel,
        out_shape=[jax.ShapeDtypeStruct(src_latent.shape, f32), jax.ShapeDtypeStruct(tgt_latent.shape, f32)],
        in_specs=[vmem] * 2,
        out_specs=[vmem] * 2,
        compiler_params=pltpu.CompilerParams(vmem_limit_bytes=4 * 2**20),
    )(mine, near)


def solution(mesh):
    spec = P(None, ("groups", "src"))
    return jax.shard_map(body, mesh=mesh, in_specs=(spec,) * 4, out_specs=(spec, spec), check_vma=False)
```

```python
import functools
import math

import jax
import jax.numpy as jnp
from jax import lax
from jax.experimental import pallas as pl
from jax.experimental.pallas import tpu as pltpu
from jax.sharding import PartitionSpec as P

SCALE = math.log2(math.e) / 0.1
LANES = 128
f32 = jnp.float32
bf16 = jnp.bfloat16


def split(value):
    high = value.astype(bf16).astype(f32)
    return high, value - high


def pack_kernel(slabs, feats, src_ref, srcp_ref, tgt_ref, tgtp_ref, out_ref, srcp_held, tgtp_held, sems):
    src_slabs = src_ref.shape[1] // LANES
    held = (srcp_held, tgtp_held)
    copies = [pltpu.make_async_copy(ref, to, sems.at[at]) for at, (ref, to) in enumerate(zip((srcp_ref, tgtp_ref), held))]
    for slab in range(slabs):
        ref, at = (src_ref, slab) if slab < src_slabs else (tgt_ref, slab - src_slabs)
        to = out_ref.at[slab * feats : (slab + 1) * feats, :]
        copies.append(pltpu.make_async_copy(ref.at[:, at * LANES : (at + 1) * LANES], to, sems.at[2 + slab]))
    for copy in copies:
        copy.start()
    out_ref[slabs * feats :, :] = jnp.zeros((out_ref.shape[0] - slabs * feats, LANES), f32)
    for copy in copies[:2]:
        copy.wait()
    for slab in range(slabs):
        pot, at = (srcp_held, slab) if slab < src_slabs else (tgtp_held, slab - src_slabs)
        for which in range(2):
            row = slabs * feats + which * slabs + slab
            out_ref[row : row + 1, :] = pot[which : which + 1, at * LANES : (at + 1) * LANES]
    for copy in copies[2:]:
        copy.wait()


def cell_terms(shape, ref, slab):
    feats, src_slabs, tgt_slabs = shape
    slabs = src_slabs + tgt_slabs
    value = ref[slab * feats : (slab + 1) * feats, :]
    norm = 0.5 * jnp.sum(value * value, 0, keepdims=True)
    first = slabs * feats + slab
    pots = [SCALE * (ref[first + which * slabs : first + which * slabs + 1, :] - norm) for which in range(2)]
    return value, pots


def store_row(shape, ref, lhs_ref, vec_ref):
    feats, src_slabs, tgt_slabs = shape
    for slab in range(src_slabs + tgt_slabs):
        value, pots = cell_terms(shape, ref, slab)
        high, low = split(value * SCALE)
        both = jnp.concatenate([high, low], 0).T.astype(bf16)
        at = slice(slab * LANES, (slab + 1) * LANES)
        lhs_ref[at, 0:LANES] = both
        lhs_ref[at, LANES:] = both
        for which in range(2):
            vec_ref[which, at, :] = jnp.broadcast_to(pots[which], (LANES, LANES)).T


def pair_kernel(shape, num_rows, num_cols, jobs, totals, prev_rows, keep, *refs):
    feats, src_slabs, tgt_slabs = shape
    slabs = src_slabs + tgt_slabs
    rows, cols = refs[:num_rows], refs[num_rows : num_rows + num_cols]
    lhs_ref, rvec_ref = refs[-2:]
    refs = refs[num_rows + num_cols : -2]
    prev, refs = refs[: len(prev_rows)], refs[len(prev_rows) :]
    outs = refs[:num_rows]
    if keep is not None:
        store_row(shape, rows[keep], *refs[num_rows:])
    sums_so_far = dict(zip(prev_rows, prev))

    row_slabs = [(row, slab) for row in range(num_rows) for slab in range(src_slabs)]
    row_slabs += [(row, slab) for row in range(num_rows) for slab in range(src_slabs, slabs)]
    for place, (row, slab) in enumerate(row_slabs):
        value, pots = cell_terms(shape, rows[row], slab)
        high, low = split(value * SCALE)
        high, low = high.astype(bf16), low.astype(bf16)
        at = slice(place * LANES, (place + 1) * LANES)
        lhs_ref[0:feats, at] = high
        lhs_ref[feats : 2 * feats, at] = high
        lhs_ref[2 * feats : 3 * feats, at] = low
        lhs_ref[3 * feats :, at] = low
        for which in range(2):
            rvec_ref[which : which + 1, at] = pots[which]

    @functools.cache
    def prepare(members):
        trans, values, vecs = [], [], []
        for col, slab in members:
            value, pots = cell_terms(shape, cols[col], slab)
            high, low = split(value)
            mid, least = split(low)
            both = jnp.concatenate([high, low], 0).T.astype(bf16)
            trans.append(jnp.concatenate([both, both], 1))
            stack = jnp.concatenate([high, mid, least, jnp.ones((16, LANES), f32)], 0)
            values.append(stack.astype(bf16))
            vecs.append(jnp.concatenate(pots + [jnp.zeros((6, LANES), f32)], 0).T)
        value = jnp.concatenate(values, 1)
        return jnp.concatenate(trans, 0), jnp.concatenate([value, value], 1), jnp.concatenate(vecs, 0)

    def run_tile(tile, prepared, own):
        row_kind = 0 if tile[0][1] < src_slabs else 1
        place = row_slabs.index(tile[0])
        at = slice(place * LANES, (place + len(tile)) * LANES)
        sums = [None, None]
        for kind, members, (trans, value, vecs) in prepared:
            which = 1 if kind == row_kind else 0
            power = jnp.dot(trans, lhs_ref[:, at], preferred_element_type=f32)
            power = power + (rvec_ref[which : which + 1, at] + vecs[:, which : which + 1])
            weight = jnp.exp2(power)
            if own and kind == row_kind:
                for down, member in enumerate(members):
                    for across, other in enumerate(tile):
                        if member == other:
                            row_id = lax.broadcasted_iota(jnp.int32, weight.shape, 0) - down * LANES
                            col_id = lax.broadcasted_iota(jnp.int32, weight.shape, 1) - across * LANES
                            same = (row_id == col_id) & (row_id >= 0) & (row_id < LANES)
                            weight = jnp.where(same, 0.0, weight)
            high, low = split(weight)
            both = jnp.concatenate([high.astype(bf16), low.astype(bf16)], 0)
            part = jnp.dot(value, both, preferred_element_type=f32)
            sums[kind] = part if sums[kind] is None else sums[kind] + part
        sign = 1.0 if row_kind == 0 else -1.0
        total = sums[1] * (sign / totals[1]) - sums[0] * (sign / totals[0])
        mixed = total[0:feats] + total[feats : 2 * feats] + total[2 * feats : 3 * feats]
        mass = total[3 * feats : 3 * feats + 1]
        for across, (row, slab) in enumerate(tile):
            piece = slice(across * LANES, (across + 1) * LANES)
            value = rows[row][slab * feats : (slab + 1) * feats, :]
            grad = value * mass[:, piece] - mixed[:, piece]
            spot = slice(slab * LANES, (slab + 1) * LANES)
            if row in sums_so_far:
                grad = grad + sums_so_far[row][:, spot]
            outs[row][:, spot] = grad

    for job_rows, job_cols, own in jobs:
        prepared = []
        for kind, first, last in ((0, 0, src_slabs), (1, src_slabs, slabs)):
            of_kind = [(col, slab) for col in job_cols for slab in range(first, last)]
            for begin in range(0, len(of_kind), 2):
                members = of_kind[begin : begin + 2]
                prepared.append((kind, members, prepare(tuple(members))))
        for first, last in ((0, src_slabs), (src_slabs, slabs)):
            of_kind = [(row, slab) for row in job_rows for slab in range(first, last)]
            for begin in range(0, len(of_kind), 2):
                run_tile(of_kind[begin : begin + 2], prepared, own)
        for row in job_rows:
            sums_so_far[row] = outs[row]


def pair_terms(shape, totals, rows, cols, prev, jobs, cost=0, keep=None):
    feats, src_slabs, tgt_slabs = shape
    width = (src_slabs + tgt_slabs) * LANES
    vmem = pl.BlockSpec(memory_space=pltpu.VMEM)
    prev_rows = [row for row, value in enumerate(prev) if value is not None]
    args = [*rows, *cols, *[prev[row] for row in prev_rows]]
    outs = [jax.ShapeDtypeStruct((feats, width), f32)] * len(rows)
    if keep is not None:
        outs += [jax.ShapeDtypeStruct((width, 4 * feats), bf16), jax.ShapeDtypeStruct((2, width, LANES), f32)]
    return pl.pallas_call(
        functools.partial(pair_kernel, shape, len(rows), len(cols), jobs, totals, prev_rows, keep),
        out_shape=outs,
        in_specs=[vmem] * len(args),
        out_specs=[vmem] * len(outs),
        scratch_shapes=[
            pltpu.VMEM((4 * feats, len(rows) * width), bf16),
            pltpu.VMEM((8, len(rows) * width), f32),
        ],
        compiler_params=pltpu.CompilerParams(vmem_limit_bytes=32 * 2**20),
        cost_estimate=pl.CostEstimate(flops=cost, bytes_accessed=2**20, transcendentals=0),
    )(*args)


def late_kernel(shape, totals, block, lhs_ref, vec_ref, col, prev, out):
    feats, src_slabs, tgt_slabs = shape
    slabs = src_slabs + tgt_slabs
    kinds = []
    for first, last in ((0, src_slabs), (src_slabs, slabs)):
        natural, values, vecs = [], [], [[], []]
        for slab in range(first, last):
            value, pots = cell_terms(shape, col, slab)
            high, low = split(value)
            mid, least = split(low)
            high, low, mid, least = (part.astype(bf16) for part in (high, low, mid, least))
            natural.append(jnp.concatenate([high, high, low, low], 0))
            values.append(jnp.concatenate([high, mid, least, jnp.ones((16, LANES), bf16)], 0))
            for which in range(2):
                vecs[which].append(pots[which])
        value = jnp.concatenate(values, 1)
        value = jnp.concatenate([value, value], 1)
        kinds.append((jnp.concatenate(natural, 1), value, [jnp.concatenate(vec, 1) for vec in vecs]))

    for row_kind, (first, last) in enumerate(((0, src_slabs), (src_slabs, slabs))):
        at = slice(first * LANES, last * LANES)
        sums = []
        for kind, (natural, value, vecs) in enumerate(kinds):
            which = 1 if kind == row_kind else 0
            power = jnp.dot(lhs_ref[at, :], natural, preferred_element_type=f32)
            spread = jnp.concatenate([vec_ref[which, at, :]] * (natural.shape[1] // LANES), 1)
            weight = jnp.exp2(power + (spread + vecs[which]))
            high, low = split(weight)
            both = jnp.concatenate([high.astype(bf16), low.astype(bf16)], 1)
            sums.append(lax.dot_general(value, both, (((1,), (1,)), ((), ())), preferred_element_type=f32))
        sign = 1.0 if row_kind == 0 else -1.0
        total = sums[1] * (sign / totals[1]) - sums[0] * (sign / totals[0])
        mixed = total[0:feats] + total[feats : 2 * feats] + total[2 * feats : 3 * feats]
        mass = total[3 * feats : 3 * feats + 1]
        for slab in range(first, last):
            piece = slice((slab - first) * LANES, (slab - first + 1) * LANES)
            spot = slice(slab * LANES, (slab + 1) * LANES)
            value = block[slab * feats : (slab + 1) * feats, :]
            out[:, spot] = value * mass[:, piece] - mixed[:, piece] + prev[:, spot]


def late_terms(shape, totals, row, col, prev):
    vmem = pl.BlockSpec(memory_space=pltpu.VMEM)
    return pl.pallas_call(
        functools.partial(late_kernel, shape, totals),
        out_shape=jax.ShapeDtypeStruct(prev.shape, f32),
        in_specs=[vmem] * 5,
        out_specs=vmem,
        compiler_params=pltpu.CompilerParams(vmem_limit_bytes=32 * 2**20),
        cost_estimate=pl.CostEstimate(flops=0, bytes_accessed=2**20, transcendentals=0),
    )(*row, col, prev)


def finish_kernel(mine_ref, near_ref, src_ref, tgt_ref):
    count = src_ref.shape[1]
    src_ref[...] = mine_ref[:, :count] + near_ref[:, :count]
    tgt_ref[...] = mine_ref[:, count:] + near_ref[:, count:]


def body(src_latent, src_potential, tgt_latent, tgt_potential):
    feats, src_count = src_latent.shape
    tgt_count = tgt_latent.shape[1]
    src_slabs, tgt_slabs = src_count // LANES, tgt_count // LANES
    shape = (feats, src_slabs, tgt_slabs)
    slabs = src_slabs + tgt_slabs
    devices = lax.axis_size("src")
    totals = (src_count * devices, tgt_count * devices)
    pot_rows = -(-2 * slabs // 8) * 8
    vmem = pl.BlockSpec(memory_space=pltpu.VMEM)
    hbm = pl.BlockSpec(memory_space=pltpu.HBM)
    args = (src_latent, src_potential, tgt_latent, tgt_potential)
    packed = pl.pallas_call(
        functools.partial(pack_kernel, slabs, feats),
        out_shape=pltpu.VMEM((slabs * feats + pot_rows, LANES), f32),
        in_specs=[hbm] * 4,
        out_specs=vmem,
        scratch_shapes=[
            pltpu.VMEM(src_potential.shape, f32),
            pltpu.VMEM(tgt_potential.shape, f32),
            pltpu.SemaphoreType.DMA((2 + slabs,)),
        ],
        compiler_params=pltpu.CompilerParams(vmem_limit_bytes=4 * 2**20),
    )(*[pltpu.with_memory_space_constraint(arg, pltpu.HBM) for arg in args])

    def swap(value, bits):
        return lax.ppermute(value, "src", [(i, i ^ bits) for i in range(devices)])

    terms = functools.partial(pair_terms, shape, totals)
    across = swap(packed, 2)
    from_z = {k: swap(packed, k) for k in range(4, devices, 4)}
    arrival = sorted(from_z, key=lambda k: (k % 8 == 0, -k))
    early, middle, last = from_z[arrival[0]], arrival[1:-1], from_z[arrival[-1]]
    near_z = from_z[middle[-1]]
    mine, *row_own = terms([packed], [packed], [None], [((0,), (0,), True)], 0, 0)
    mine = late_terms(shape, totals, (packed, *row_own), early, mine)
    mine, later, again = lax.optimization_barrier((mine, across, packed))
    corner = swap(later, 1)
    beside = swap(again, 1)
    wide, *row_later = terms([later], [packed, early], [None], [((0,), (0, 1), False)], 10**10, 0)
    near = None
    corner, beside, wide = lax.optimization_barrier((corner, beside, wide))
    near, sent, *row_corner = terms([beside, corner], [packed, early], [None] * 2, [((0, 1), (0, 1), False)], 0, 1)
    wide, sent = terms([across, corner], [near_z], [wide, sent], [((0, 1), (0,), False)])
    for at in range(0, len(middle) - 1, 2):
        group = [from_z[k] for k in middle[at : min(at + 2, len(middle) - 1)]]
        jobs = [((0, 1, 2, 3), tuple(range(len(group))), False)]
        mine, near, wide, sent = terms([packed, beside, across, corner], group, [mine, near, wide, sent], jobs)
    sent = late_terms(shape, totals, (corner, *row_corner), last, sent)
    got = swap(sent, 1)
    wide = late_terms(shape, totals, (across, *row_later), last, wide)
    send = wide + got
    far = swap(send, 2)
    last, send = lax.optimization_barrier((last, send))
    mine, near = terms([packed, beside], [near_z, last], [mine, near], [((0, 1), (0, 1), False)])
    near = swap(near, 1)
    mine = mine + far
    return pl.pallas_call(
        finish_kernel,
        out_shape=[jax.ShapeDtypeStruct(src_latent.shape, f32), jax.ShapeDtypeStruct(tgt_latent.shape, f32)],
        in_specs=[vmem] * 2,
        out_specs=[vmem] * 2,
        compiler_params=pltpu.CompilerParams(vmem_limit_bytes=4 * 2**20),
    )(mine, near)


def solution(mesh):
    spec = P(None, ("groups", "src"))
    return jax.shard_map(body, mesh=mesh, in_specs=(spec,) * 4, out_specs=(spec, spec), check_vma=False)
```

```python
import functools
import math

import jax
import jax.numpy as jnp
from jax import lax
from jax.experimental import pallas as pl
from jax.experimental.pallas import tpu as pltpu
from jax.sharding import PartitionSpec as P

SCALE = math.log2(math.e) / 0.1
LANES = 128
f32 = jnp.float32
bf16 = jnp.bfloat16


def split(value):
    high = value.astype(bf16).astype(f32)
    return high, value - high


def pack_kernel(slabs, feats, src_ref, srcp_ref, tgt_ref, tgtp_ref, out_ref, srcp_held, tgtp_held, sems):
    src_slabs = src_ref.shape[1] // LANES
    held = (srcp_held, tgtp_held)
    copies = [pltpu.make_async_copy(ref, to, sems.at[at]) for at, (ref, to) in enumerate(zip((srcp_ref, tgtp_ref), held))]
    for slab in range(slabs):
        ref, at = (src_ref, slab) if slab < src_slabs else (tgt_ref, slab - src_slabs)
        to = out_ref.at[slab * feats : (slab + 1) * feats, :]
        copies.append(pltpu.make_async_copy(ref.at[:, at * LANES : (at + 1) * LANES], to, sems.at[2 + slab]))
    for copy in copies:
        copy.start()
    out_ref[slabs * feats :, :] = jnp.zeros((out_ref.shape[0] - slabs * feats, LANES), f32)
    for copy in copies[:2]:
        copy.wait()
    for slab in range(slabs):
        pot, at = (srcp_held, slab) if slab < src_slabs else (tgtp_held, slab - src_slabs)
        for which in range(2):
            row = slabs * feats + which * slabs + slab
            out_ref[row : row + 1, :] = pot[which : which + 1, at * LANES : (at + 1) * LANES]
    for copy in copies[2:]:
        copy.wait()


def cell_terms(shape, ref, slab):
    feats, src_slabs, tgt_slabs = shape
    slabs = src_slabs + tgt_slabs
    value = ref[slab * feats : (slab + 1) * feats, :]
    norm = 0.5 * jnp.sum(value * value, 0, keepdims=True)
    first = slabs * feats + slab
    pots = [SCALE * (ref[first + which * slabs : first + which * slabs + 1, :] - norm) for which in range(2)]
    return value, pots


def store_row(shape, ref, lhs_ref, vec_ref):
    feats, src_slabs, tgt_slabs = shape
    for slab in range(src_slabs + tgt_slabs):
        value, pots = cell_terms(shape, ref, slab)
        high, low = split(value * SCALE)
        both = jnp.concatenate([high, low], 0).T.astype(bf16)
        at = slice(slab * LANES, (slab + 1) * LANES)
        lhs_ref[at, 0:LANES] = both
        lhs_ref[at, LANES:] = both
        for which in range(2):
            vec_ref[which, at, :] = jnp.broadcast_to(pots[which], (LANES, LANES)).T


def pair_kernel(shape, num_rows, num_cols, jobs, totals, prev_rows, keep, *refs):
    feats, src_slabs, tgt_slabs = shape
    slabs = src_slabs + tgt_slabs
    rows, cols = refs[:num_rows], refs[num_rows : num_rows + num_cols]
    lhs_ref, rvec_ref = refs[-2:]
    refs = refs[num_rows + num_cols : -2]
    prev, refs = refs[: len(prev_rows)], refs[len(prev_rows) :]
    outs = refs[:num_rows]
    if keep is not None:
        store_row(shape, rows[keep], *refs[num_rows:])
    sums_so_far = dict(zip(prev_rows, prev))

    row_slabs = [(row, slab) for row in range(num_rows) for slab in range(src_slabs)]
    row_slabs += [(row, slab) for row in range(num_rows) for slab in range(src_slabs, slabs)]
    for place, (row, slab) in enumerate(row_slabs):
        value, pots = cell_terms(shape, rows[row], slab)
        high, low = split(value * SCALE)
        high, low = high.astype(bf16), low.astype(bf16)
        at = slice(place * LANES, (place + 1) * LANES)
        lhs_ref[0:feats, at] = high
        lhs_ref[feats : 2 * feats, at] = high
        lhs_ref[2 * feats : 3 * feats, at] = low
        lhs_ref[3 * feats :, at] = low
        for which in range(2):
            rvec_ref[which : which + 1, at] = pots[which]

    @functools.cache
    def prepare(members):
        trans, values, vecs = [], [], []
        for col, slab in members:
            value, pots = cell_terms(shape, cols[col], slab)
            high, low = split(value)
            mid, least = split(low)
            both = jnp.concatenate([high, low], 0).T.astype(bf16)
            trans.append(jnp.concatenate([both, both], 1))
            stack = jnp.concatenate([high, mid, jnp.ones((16, LANES), f32), least], 0)
            values.append(stack.astype(bf16))
            vecs.append(jnp.concatenate(pots + [jnp.zeros((6, LANES), f32)], 0).T)
        value = jnp.concatenate(values, 1)
        return jnp.concatenate(trans, 0), value, jnp.concatenate(vecs, 0)

    def run_tile(tile, prepared, own):
        row_kind = 0 if tile[0][1] < src_slabs else 1
        place = row_slabs.index(tile[0])
        at = slice(place * LANES, (place + len(tile)) * LANES)
        sums = [None, None]
        for kind, members, (trans, value, vecs) in prepared:
            which = 1 if kind == row_kind else 0
            power = jnp.dot(trans, lhs_ref[:, at], preferred_element_type=f32)
            power = power + (rvec_ref[which : which + 1, at] + vecs[:, which : which + 1])
            weight = jnp.exp2(power)
            if own and kind == row_kind:
                for down, member in enumerate(members):
                    for across, other in enumerate(tile):
                        if member == other:
                            row_id = lax.broadcasted_iota(jnp.int32, weight.shape, 0) - down * LANES
                            col_id = lax.broadcasted_iota(jnp.int32, weight.shape, 1) - across * LANES
                            same = (row_id == col_id) & (row_id >= 0) & (row_id < LANES)
                            weight = jnp.where(same, 0.0, weight)
            high, low = split(weight)
            part = jnp.dot(value, high.astype(bf16), preferred_element_type=f32)
            most = 2 * feats + 16
            fine = jnp.dot(value[:most], low.astype(bf16), preferred_element_type=f32)
            part = jnp.concatenate([part[:most] + fine, part[most:]], 0)
            sums[kind] = part if sums[kind] is None else sums[kind] + part
        sign = 1.0 if row_kind == 0 else -1.0
        total = sums[1] * (sign / totals[1]) - sums[0] * (sign / totals[0])
        mixed = total[0:feats] + total[feats : 2 * feats] + total[2 * feats + 16 :]
        mass = total[2 * feats : 2 * feats + 1]
        for across, (row, slab) in enumerate(tile):
            piece = slice(across * LANES, (across + 1) * LANES)
            value = rows[row][slab * feats : (slab + 1) * feats, :]
            grad = value * mass[:, piece] - mixed[:, piece]
            spot = slice(slab * LANES, (slab + 1) * LANES)
            if row in sums_so_far:
                grad = grad + sums_so_far[row][:, spot]
            outs[row][:, spot] = grad

    for job_rows, job_cols, own in jobs:
        prepared = []
        for kind, first, last in ((0, 0, src_slabs), (1, src_slabs, slabs)):
            of_kind = [(col, slab) for col in job_cols for slab in range(first, last)]
            for begin in range(0, len(of_kind), 2):
                members = of_kind[begin : begin + 2]
                prepared.append((kind, members, prepare(tuple(members))))
        for first, last in ((0, src_slabs), (src_slabs, slabs)):
            of_kind = [(row, slab) for row in job_rows for slab in range(first, last)]
            for begin in range(0, len(of_kind), 2):
                run_tile(of_kind[begin : begin + 2], prepared, own)
        for row in job_rows:
            sums_so_far[row] = outs[row]


def pair_terms(shape, totals, rows, cols, prev, jobs, cost=0, keep=None):
    feats, src_slabs, tgt_slabs = shape
    width = (src_slabs + tgt_slabs) * LANES
    vmem = pl.BlockSpec(memory_space=pltpu.VMEM)
    prev_rows = [row for row, value in enumerate(prev) if value is not None]
    args = [*rows, *cols, *[prev[row] for row in prev_rows]]
    outs = [jax.ShapeDtypeStruct((feats, width), f32)] * len(rows)
    if keep is not None:
        outs += [jax.ShapeDtypeStruct((width, 4 * feats), bf16), jax.ShapeDtypeStruct((2, width, LANES), f32)]
    return pl.pallas_call(
        functools.partial(pair_kernel, shape, len(rows), len(cols), jobs, totals, prev_rows, keep),
        out_shape=outs,
        in_specs=[vmem] * len(args),
        out_specs=[vmem] * len(outs),
        scratch_shapes=[
            pltpu.VMEM((4 * feats, len(rows) * width), bf16),
            pltpu.VMEM((8, len(rows) * width), f32),
        ],
        compiler_params=pltpu.CompilerParams(vmem_limit_bytes=32 * 2**20),
        cost_estimate=pl.CostEstimate(flops=cost, bytes_accessed=2**20, transcendentals=0),
    )(*args)


def late_kernel(shape, totals, block, lhs_ref, vec_ref, col, prev, out):
    feats, src_slabs, tgt_slabs = shape
    slabs = src_slabs + tgt_slabs
    kinds = []
    for first, last in ((0, src_slabs), (src_slabs, slabs)):
        natural, values, vecs = [], [], [[], []]
        for slab in range(first, last):
            value, pots = cell_terms(shape, col, slab)
            high, low = split(value)
            mid, least = split(low)
            high, low, mid, least = (part.astype(bf16) for part in (high, low, mid, least))
            natural.append(jnp.concatenate([high, high, low, low], 0))
            values.append(jnp.concatenate([high, mid, least, jnp.ones((16, LANES), bf16)], 0))
            for which in range(2):
                vecs[which].append(pots[which])
        value = jnp.concatenate(values, 1)
        value = jnp.concatenate([value, value], 1)
        kinds.append((jnp.concatenate(natural, 1), value, [jnp.concatenate(vec, 1) for vec in vecs]))

    for row_kind, (first, last) in enumerate(((0, src_slabs), (src_slabs, slabs))):
        at = slice(first * LANES, last * LANES)
        sums = []
        for kind, (natural, value, vecs) in enumerate(kinds):
            which = 1 if kind == row_kind else 0
            power = jnp.dot(lhs_ref[at, :], natural, preferred_element_type=f32)
            spread = jnp.concatenate([vec_ref[which, at, :]] * (natural.shape[1] // LANES), 1)
            weight = jnp.exp2(power + (spread + vecs[which]))
            high, low = split(weight)
            both = jnp.concatenate([high.astype(bf16), low.astype(bf16)], 1)
            sums.append(lax.dot_general(value, both, (((1,), (1,)), ((), ())), preferred_element_type=f32))
        sign = 1.0 if row_kind == 0 else -1.0
        total = sums[1] * (sign / totals[1]) - sums[0] * (sign / totals[0])
        mixed = total[0:feats] + total[feats : 2 * feats] + total[2 * feats : 3 * feats]
        mass = total[3 * feats : 3 * feats + 1]
        for slab in range(first, last):
            piece = slice((slab - first) * LANES, (slab - first + 1) * LANES)
            spot = slice(slab * LANES, (slab + 1) * LANES)
            value = block[slab * feats : (slab + 1) * feats, :]
            out[:, spot] = value * mass[:, piece] - mixed[:, piece] + prev[:, spot]


def late_terms(shape, totals, row, col, prev):
    vmem = pl.BlockSpec(memory_space=pltpu.VMEM)
    return pl.pallas_call(
        functools.partial(late_kernel, shape, totals),
        out_shape=jax.ShapeDtypeStruct(prev.shape, f32),
        in_specs=[vmem] * 5,
        out_specs=vmem,
        compiler_params=pltpu.CompilerParams(vmem_limit_bytes=32 * 2**20),
        cost_estimate=pl.CostEstimate(flops=0, bytes_accessed=2**20, transcendentals=0),
    )(*row, col, prev)


def finish_kernel(mine_ref, near_ref, src_ref, tgt_ref):
    count = src_ref.shape[1]
    src_ref[...] = mine_ref[:, :count] + near_ref[:, :count]
    tgt_ref[...] = mine_ref[:, count:] + near_ref[:, count:]


def body(src_latent, src_potential, tgt_latent, tgt_potential):
    feats, src_count = src_latent.shape
    tgt_count = tgt_latent.shape[1]
    src_slabs, tgt_slabs = src_count // LANES, tgt_count // LANES
    shape = (feats, src_slabs, tgt_slabs)
    slabs = src_slabs + tgt_slabs
    devices = lax.axis_size("src")
    totals = (src_count * devices, tgt_count * devices)
    pot_rows = -(-2 * slabs // 8) * 8
    vmem = pl.BlockSpec(memory_space=pltpu.VMEM)
    hbm = pl.BlockSpec(memory_space=pltpu.HBM)
    args = (src_latent, src_potential, tgt_latent, tgt_potential)
    packed = pl.pallas_call(
        functools.partial(pack_kernel, slabs, feats),
        out_shape=pltpu.VMEM((slabs * feats + pot_rows, LANES), f32),
        in_specs=[hbm] * 4,
        out_specs=vmem,
        scratch_shapes=[
            pltpu.VMEM(src_potential.shape, f32),
            pltpu.VMEM(tgt_potential.shape, f32),
            pltpu.SemaphoreType.DMA((2 + slabs,)),
        ],
        compiler_params=pltpu.CompilerParams(vmem_limit_bytes=4 * 2**20),
    )(*[pltpu.with_memory_space_constraint(arg, pltpu.HBM) for arg in args])

    def swap(value, bits):
        return lax.ppermute(value, "src", [(i, i ^ bits) for i in range(devices)])

    terms = functools.partial(pair_terms, shape, totals)
    across = swap(packed, 2)
    from_z = {k: swap(packed, k) for k in range(4, devices, 4)}
    arrival = sorted(from_z, key=lambda k: (k % 8 == 0, -k))
    early, middle, last = from_z[arrival[0]], arrival[1:-1], from_z[arrival[-1]]
    near_z = from_z[middle[-1]]
    mine, *row_own = terms([packed], [packed], [None], [((0,), (0,), True)], 0, 0)
    mine = late_terms(shape, totals, (packed, *row_own), early, mine)
    mine, later, again = lax.optimization_barrier((mine, across, packed))
    corner = swap(later, 1)
    beside = swap(again, 1)
    wide, *row_later = terms([later], [packed, early], [None], [((0,), (0, 1), False)], 10**10, 0)
    near = None
    corner, beside, wide = lax.optimization_barrier((corner, beside, wide))
    near, sent, *row_corner = terms([beside, corner], [packed, early], [None] * 2, [((0, 1), (0, 1), False)], 0, 1)
    wide, sent = terms([across, corner], [near_z], [wide, sent], [((0, 1), (0,), False)])
    for at in range(0, len(middle) - 1, 2):
        group = [from_z[k] for k in middle[at : min(at + 2, len(middle) - 1)]]
        jobs = [((0, 1, 2, 3), tuple(range(len(group))), False)]
        mine, near, wide, sent = terms([packed, beside, across, corner], group, [mine, near, wide, sent], jobs)
    sent = late_terms(shape, totals, (corner, *row_corner), last, sent)
    got = swap(sent, 1)
    wide = late_terms(shape, totals, (across, *row_later), last, wide)
    send = wide + got
    far = swap(send, 2)
    last, send = lax.optimization_barrier((last, send))
    mine, near = terms([packed, beside], [near_z, last], [mine, near], [((0, 1), (0, 1), False)])
    near = swap(near, 1)
    mine = mine + far
    return pl.pallas_call(
        finish_kernel,
        out_shape=[jax.ShapeDtypeStruct(src_latent.shape, f32), jax.ShapeDtypeStruct(tgt_latent.shape, f32)],
        in_specs=[vmem] * 2,
        out_specs=[vmem] * 2,
        compiler_params=pltpu.CompilerParams(vmem_limit_bytes=4 * 2**20),
    )(mine, near)


def solution(mesh):
    spec = P(None, ("groups", "src"))
    return jax.shard_map(body, mesh=mesh, in_specs=(spec,) * 4, out_specs=(spec, spec), check_vma=False)
```

```python
import functools
import math

import jax
import jax.numpy as jnp
from jax import lax
from jax.experimental import pallas as pl
from jax.experimental.pallas import tpu as pltpu
from jax.sharding import PartitionSpec as P

SCALE = math.log2(math.e) / 0.1
LANES = 128
f32 = jnp.float32
bf16 = jnp.bfloat16


def split(value):
    high = value.astype(bf16).astype(f32)
    return high, value - high


def pack_kernel(slabs, feats, src_ref, srcp_ref, tgt_ref, tgtp_ref, out_ref, srcp_held, tgtp_held, sems):
    src_slabs = src_ref.shape[1] // LANES
    held = (srcp_held, tgtp_held)
    copies = [pltpu.make_async_copy(ref, to, sems.at[at]) for at, (ref, to) in enumerate(zip((srcp_ref, tgtp_ref), held))]
    for slab in range(slabs):
        ref, at = (src_ref, slab) if slab < src_slabs else (tgt_ref, slab - src_slabs)
        to = out_ref.at[slab * feats : (slab + 1) * feats, :]
        copies.append(pltpu.make_async_copy(ref.at[:, at * LANES : (at + 1) * LANES], to, sems.at[2 + slab]))
    for copy in copies:
        copy.start()
    out_ref[slabs * feats :, :] = jnp.zeros((out_ref.shape[0] - slabs * feats, LANES), f32)
    for copy in copies[:2]:
        copy.wait()
    for slab in range(slabs):
        pot, at = (srcp_held, slab) if slab < src_slabs else (tgtp_held, slab - src_slabs)
        for which in range(2):
            row = slabs * feats + which * slabs + slab
            out_ref[row : row + 1, :] = pot[which : which + 1, at * LANES : (at + 1) * LANES]
    for copy in copies[2:]:
        copy.wait()


def cell_terms(shape, ref, slab):
    feats, src_slabs, tgt_slabs = shape
    slabs = src_slabs + tgt_slabs
    value = ref[slab * feats : (slab + 1) * feats, :]
    norm = 0.5 * jnp.sum(value * value, 0, keepdims=True)
    first = slabs * feats + slab
    pots = [SCALE * (ref[first + which * slabs : first + which * slabs + 1, :] - norm) for which in range(2)]
    return value, pots


def store_row(shape, ref, lhs_ref, vec_ref):
    feats, src_slabs, tgt_slabs = shape
    for slab in range(src_slabs + tgt_slabs):
        value, pots = cell_terms(shape, ref, slab)
        high, low = split(value * SCALE)
        both = jnp.concatenate([high, low], 0).T.astype(bf16)
        at = slice(slab * LANES, (slab + 1) * LANES)
        lhs_ref[at, 0:LANES] = both
        lhs_ref[at, LANES:] = both
        for which in range(2):
            vec_ref[which, at, :] = jnp.broadcast_to(pots[which], (LANES, LANES)).T


def pair_kernel(shape, num_rows, num_cols, jobs, totals, prev_rows, keep, *refs):
    feats, src_slabs, tgt_slabs = shape
    slabs = src_slabs + tgt_slabs
    rows, cols = refs[:num_rows], refs[num_rows : num_rows + num_cols]
    lhs_ref, rvec_ref = refs[-2:]
    refs = refs[num_rows + num_cols : -2]
    prev, refs = refs[: len(prev_rows)], refs[len(prev_rows) :]
    outs = refs[:num_rows]
    if keep is not None:
        store_row(shape, rows[keep], *refs[num_rows:])
    sums_so_far = dict(zip(prev_rows, prev))

    row_slabs = [(row, slab) for row in range(num_rows) for slab in range(src_slabs)]
    row_slabs += [(row, slab) for row in range(num_rows) for slab in range(src_slabs, slabs)]
    for place, (row, slab) in enumerate(row_slabs):
        value, pots = cell_terms(shape, rows[row], slab)
        high, low = split(value * SCALE)
        high, low = high.astype(bf16), low.astype(bf16)
        at = slice(place * LANES, (place + 1) * LANES)
        lhs_ref[0:feats, at] = high
        lhs_ref[feats : 2 * feats, at] = high
        lhs_ref[2 * feats : 3 * feats, at] = low
        lhs_ref[3 * feats :, at] = low
        for which in range(2):
            rvec_ref[which : which + 1, at] = pots[which]

    @functools.cache
    def prepare(members):
        trans, values, vecs = [], [], []
        for col, slab in members:
            value, pots = cell_terms(shape, cols[col], slab)
            high, low = split(value)
            mid, least = split(low)
            both = jnp.concatenate([high, low], 0).T.astype(bf16)
            trans.append(jnp.concatenate([both, both], 1))
            stack = jnp.concatenate([high, mid, jnp.ones((16, LANES), f32), least], 0)
            values.append(stack.astype(bf16))
            vecs.append(jnp.concatenate(pots + [jnp.zeros((6, LANES), f32)], 0).T)
        value = jnp.concatenate(values, 1)
        return jnp.concatenate(trans, 0), value, jnp.concatenate(vecs, 0)

    def run_tile(tile, prepared, own):
        row_kind = 0 if tile[0][1] < src_slabs else 1
        place = row_slabs.index(tile[0])
        at = slice(place * LANES, (place + len(tile)) * LANES)
        sums = [None, None]
        for kind, members, (trans, value, vecs) in prepared:
            which = 1 if kind == row_kind else 0
            power = jnp.dot(trans, lhs_ref[:, at], preferred_element_type=f32)
            power = power + (rvec_ref[which : which + 1, at] + vecs[:, which : which + 1])
            weight = jnp.exp2(power)
            if own and kind == row_kind:
                for down, member in enumerate(members):
                    for across, other in enumerate(tile):
                        if member == other:
                            row_id = lax.broadcasted_iota(jnp.int32, weight.shape, 0) - down * LANES
                            col_id = lax.broadcasted_iota(jnp.int32, weight.shape, 1) - across * LANES
                            same = (row_id == col_id) & (row_id >= 0) & (row_id < LANES)
                            weight = jnp.where(same, 0.0, weight)
            high, low = split(weight)
            part = jnp.dot(value, high.astype(bf16), preferred_element_type=f32)
            most = 2 * feats + 16
            fine = jnp.dot(value[:most], low.astype(bf16), preferred_element_type=f32)
            part = jnp.concatenate([part[:most] + fine, part[most:]], 0)
            sums[kind] = part if sums[kind] is None else sums[kind] + part
        sign = 1.0 if row_kind == 0 else -1.0
        total = sums[1] * (sign / totals[1]) - sums[0] * (sign / totals[0])
        mixed = total[0:feats] + total[feats : 2 * feats] + total[2 * feats + 16 :]
        mass = total[2 * feats : 2 * feats + 1]
        for across, (row, slab) in enumerate(tile):
            piece = slice(across * LANES, (across + 1) * LANES)
            value = rows[row][slab * feats : (slab + 1) * feats, :]
            grad = value * mass[:, piece] - mixed[:, piece]
            spot = slice(slab * LANES, (slab + 1) * LANES)
            if row in sums_so_far:
                grad = grad + sums_so_far[row][:, spot]
            outs[row][:, spot] = grad

    for job_rows, job_cols, own in jobs:
        prepared = []
        for kind, first, last in ((0, 0, src_slabs), (1, src_slabs, slabs)):
            of_kind = [(col, slab) for col in job_cols for slab in range(first, last)]
            for begin in range(0, len(of_kind), 2):
                members = of_kind[begin : begin + 2]
                prepared.append((kind, members, prepare(tuple(members))))
        for first, last in ((0, src_slabs), (src_slabs, slabs)):
            of_kind = [(row, slab) for row in job_rows for slab in range(first, last)]
            for begin in range(0, len(of_kind), 2):
                run_tile(of_kind[begin : begin + 2], prepared, own)
        for row in job_rows:
            sums_so_far[row] = outs[row]


def pair_terms(shape, totals, rows, cols, prev, jobs, cost=0, keep=None):
    feats, src_slabs, tgt_slabs = shape
    width = (src_slabs + tgt_slabs) * LANES
    vmem = pl.BlockSpec(memory_space=pltpu.VMEM)
    prev_rows = [row for row, value in enumerate(prev) if value is not None]
    args = [*rows, *cols, *[prev[row] for row in prev_rows]]
    outs = [jax.ShapeDtypeStruct((feats, width), f32)] * len(rows)
    if keep is not None:
        outs += [jax.ShapeDtypeStruct((width, 4 * feats), bf16), jax.ShapeDtypeStruct((2, width, LANES), f32)]
    return pl.pallas_call(
        functools.partial(pair_kernel, shape, len(rows), len(cols), jobs, totals, prev_rows, keep),
        out_shape=outs,
        in_specs=[vmem] * len(args),
        out_specs=[vmem] * len(outs),
        scratch_shapes=[
            pltpu.VMEM((4 * feats, len(rows) * width), bf16),
            pltpu.VMEM((8, len(rows) * width), f32),
        ],
        compiler_params=pltpu.CompilerParams(vmem_limit_bytes=32 * 2**20),
        cost_estimate=pl.CostEstimate(flops=cost, bytes_accessed=2**20, transcendentals=0),
    )(*args)


def late_kernel(shape, totals, block, lhs_ref, vec_ref, col, prev, out):
    feats, src_slabs, tgt_slabs = shape
    slabs = src_slabs + tgt_slabs
    kinds = []
    for first, last in ((0, src_slabs), (src_slabs, slabs)):
        natural, values, vecs = [], [], [[], []]
        for slab in range(first, last):
            value, pots = cell_terms(shape, col, slab)
            high, low = split(value)
            mid, least = split(low)
            high, low, mid, least = (part.astype(bf16) for part in (high, low, mid, least))
            natural.append(jnp.concatenate([high, high, low, low], 0))
            values.append(jnp.concatenate([high, mid, least, jnp.ones((16, LANES), bf16)], 0))
            for which in range(2):
                vecs[which].append(pots[which])
        value = jnp.concatenate(values, 1)
        value = jnp.concatenate([value, value], 1)
        kinds.append((jnp.concatenate(natural, 1), value, [jnp.concatenate(vec, 1) for vec in vecs]))

    for row_kind, (first, last) in enumerate(((0, src_slabs), (src_slabs, slabs))):
        at = slice(first * LANES, last * LANES)
        sums = []
        for kind, (natural, value, vecs) in enumerate(kinds):
            which = 1 if kind == row_kind else 0
            power = jnp.dot(lhs_ref[at, :], natural, preferred_element_type=f32)
            spread = jnp.concatenate([vec_ref[which, at, :]] * (natural.shape[1] // LANES), 1)
            weight = jnp.exp2(power + (spread + vecs[which]))
            high, low = split(weight)
            both = jnp.concatenate([high.astype(bf16), low.astype(bf16)], 1)
            sums.append(lax.dot_general(value, both, (((1,), (1,)), ((), ())), preferred_element_type=f32))
        sign = 1.0 if row_kind == 0 else -1.0
        total = sums[1] * (sign / totals[1]) - sums[0] * (sign / totals[0])
        mixed = total[0:feats] + total[feats : 2 * feats] + total[2 * feats : 3 * feats]
        mass = total[3 * feats : 3 * feats + 1]
        for slab in range(first, last):
            piece = slice((slab - first) * LANES, (slab - first + 1) * LANES)
            spot = slice(slab * LANES, (slab + 1) * LANES)
            value = block[slab * feats : (slab + 1) * feats, :]
            out[:, spot] = value * mass[:, piece] - mixed[:, piece] + prev[:, spot]


def late_terms(shape, totals, row, col, prev):
    vmem = pl.BlockSpec(memory_space=pltpu.VMEM)
    return pl.pallas_call(
        functools.partial(late_kernel, shape, totals),
        out_shape=jax.ShapeDtypeStruct(prev.shape, f32),
        in_specs=[vmem] * 5,
        out_specs=vmem,
        compiler_params=pltpu.CompilerParams(vmem_limit_bytes=32 * 2**20),
        cost_estimate=pl.CostEstimate(flops=0, bytes_accessed=2**20, transcendentals=0),
    )(*row, col, prev)


def finish_kernel(mine_ref, far_ref, near_ref, src_ref, tgt_ref):
    count = src_ref.shape[1]
    src_ref[...] = mine_ref[:, :count] + far_ref[:, :count] + near_ref[:, :count]
    tgt_ref[...] = mine_ref[:, count:] + far_ref[:, count:] + near_ref[:, count:]


def body(src_latent, src_potential, tgt_latent, tgt_potential):
    feats, src_count = src_latent.shape
    tgt_count = tgt_latent.shape[1]
    src_slabs, tgt_slabs = src_count // LANES, tgt_count // LANES
    shape = (feats, src_slabs, tgt_slabs)
    slabs = src_slabs + tgt_slabs
    devices = lax.axis_size("src")
    totals = (src_count * devices, tgt_count * devices)
    pot_rows = -(-2 * slabs // 8) * 8
    vmem = pl.BlockSpec(memory_space=pltpu.VMEM)
    hbm = pl.BlockSpec(memory_space=pltpu.HBM)
    args = (src_latent, src_potential, tgt_latent, tgt_potential)
    packed = pl.pallas_call(
        functools.partial(pack_kernel, slabs, feats),
        out_shape=pltpu.VMEM((slabs * feats + pot_rows, LANES), f32),
        in_specs=[hbm] * 4,
        out_specs=vmem,
        scratch_shapes=[
            pltpu.VMEM(src_potential.shape, f32),
            pltpu.VMEM(tgt_potential.shape, f32),
            pltpu.SemaphoreType.DMA((2 + slabs,)),
        ],
        compiler_params=pltpu.CompilerParams(vmem_limit_bytes=4 * 2**20),
    )(*[pltpu.with_memory_space_constraint(arg, pltpu.HBM) for arg in args])

    def swap(value, bits):
        return lax.ppermute(value, "src", [(i, i ^ bits) for i in range(devices)])

    terms = functools.partial(pair_terms, shape, totals)
    across = swap(packed, 2)
    from_z = {k: swap(packed, k) for k in range(4, devices, 4)}
    arrival = sorted(from_z, key=lambda k: (k % 8 == 0, -k))
    early, middle, last = from_z[arrival[0]], arrival[1:-1], from_z[arrival[-1]]
    near_z = from_z[middle[-1]]
    mine, *row_own = terms([packed], [packed], [None], [((0,), (0,), True)], 0, 0)
    mine = late_terms(shape, totals, (packed, *row_own), early, mine)
    mine, later, again = lax.optimization_barrier((mine, across, packed))
    corner = swap(later, 1)
    beside = swap(again, 1)
    wide, *row_later = terms([later], [packed, early], [None], [((0,), (0, 1), False)], 10**10, 0)
    near = None
    corner, beside, wide = lax.optimization_barrier((corner, beside, wide))
    near, sent, *row_corner = terms([beside, corner], [packed, early], [None] * 2, [((0, 1), (0, 1), False)], 0, 1)
    wide, sent = terms([across, corner], [near_z], [wide, sent], [((0, 1), (0,), False)])
    for at in range(0, len(middle) - 1, 2):
        group = [from_z[k] for k in middle[at : min(at + 2, len(middle) - 1)]]
        jobs = [((0, 1, 2, 3), tuple(range(len(group))), False)]
        mine, near, wide, sent = terms([packed, beside, across, corner], group, [mine, near, wide, sent], jobs)
    sent = late_terms(shape, totals, (corner, *row_corner), last, sent)
    got = swap(sent, 1)
    wide = late_terms(shape, totals, (across, *row_later), last, wide)
    send = wide + got
    far = swap(send, 2)
    last, send = lax.optimization_barrier((last, send))
    mine, near = terms([packed, beside], [near_z, last], [mine, near], [((0, 1), (0, 1), False)])
    near = swap(near, 1)
    return pl.pallas_call(
        finish_kernel,
        out_shape=[jax.ShapeDtypeStruct(src_latent.shape, f32), jax.ShapeDtypeStruct(tgt_latent.shape, f32)],
        in_specs=[vmem] * 3,
        out_specs=[vmem] * 2,
        compiler_params=pltpu.CompilerParams(vmem_limit_bytes=4 * 2**20),
    )(mine, far, near)


def solution(mesh):
    spec = P(None, ("groups", "src"))
    return jax.shard_map(body, mesh=mesh, in_specs=(spec,) * 4, out_specs=(spec, spec), check_vma=False)
```
